128 devices in a mesh: bx: 8 (over x, core), by: 16 (over y, z).
Axes of the slice: x: 4, y: 4, z: 4, core: 2. Of those that a mesh axis runs over, the one named last changes fastest.
Arguments:
- tetrahedron_defect_values: float32 [1048576], P(('bx', 'by')), may hold values from -6 to 6
- tetrahedron_destination_block: int32 [1048576, 1], P(('bx', 'by')), may hold values from 0 to 127; in each aligned block of 8192 rows (0 to 8191, 8192 to 16383, ...) at most 96 rows name the same one
- active_entries_per_part: int32 [128], P(('bx', 'by')), may hold values from 1 to 8192, 786432 in all
- corner_factor_block_index: int32 [4, 1572864], P(None, ('bx', 'by')), may hold values from 0 to 511
- corner_factor_elevation: int32 [4, 1572864], P(None, ('bx', 'by')), may hold values from 0 to 255
- corner_interpolation_factors: float32 [4, 1572864], P(None, ('bx', 'by')), may hold values from 0.1 to 1
- baseline_heat_coefficient: float32 [128, 512, 256], P('bx', 'by'), may hold values from 0.5 to 5
- thermal_state_iterate: float32 [128, 512, 256], P('bx', 'by'), may hold values from -3 to 3
Outputs:
- grid_correction: float32 [128, 512, 256], P('bx', 'by')
- tet_correction: float32 [1048576], P(('bx', 'by'))
The draws below stay inside these ranges and needn't reach their ends.
Inputs may be any that keep to these rules, and one draw needn't show every extreme that they name: `tetrahedron_destination_block`: among the 8192 rows of one device no brick is named more than 96 times, a bound that some block reaches. `active_entries_per_part`: some device has all 8192 rows live.
All inputs are finite; a program needn't handle non-finite values.
Results may differ from the reference program's by a relative error of at most 0.0003.
Values sent between devices are 32-bit elements; how exact they have to be, the bound alone decides.
No kernel may reach another device: no remote copies, remote signals or barrier semaphores. Data moves between devices by JAX's collectives and lax.ppermute only.
A program may use at most 128 MiB of HBM per device.

```python
import math
import jax
import jax.numpy as jnp
import numpy as np
from jax import lax

CX = 16
CY = 32
SPAN_ALONG_Z = 256
TET_DEV = 8192
LEVELS = 3
NU = 3
CSWEEPS = 8
SPAN_ALONG_X = 128
SPAN_ALONG_Y = 512
TETS = 1048576
CAP = 96
SLOTS = 1572864
N_BX = 8
N_BY = 16
DEVICES = 128


def touch_ends(drawn, stream_key, smallest, top_value):
    place = [jax.random.randint(jax.random.fold_in(stream_key, axis), (), 0, length) for axis, length in enumerate(drawn.shape)]
    widest = drawn.shape.index(max(drawn.shape))
    neighbour = place[:widest] + [(place[widest] + 1) % drawn.shape[widest]] + place[widest + 1:]
    return drawn.at[tuple(place)].set(smallest).at[tuple(neighbour)].set(top_value)


def block_levels(rng, shape, shards, low, largest):
    level = 1.0
    for axis_at, shards_of in shards:
        heights = jax.random.uniform(jax.random.fold_in(jax.random.fold_in(rng, 6), axis_at), (shards_of,), jnp.float32, low / len(shards), largest / len(shards))
        level = level * jnp.repeat(jnp.exp(heights), shape[axis_at] // shards_of).reshape((-1,) + (1,) * (len(shape) - 1 - axis_at))
    return level


def profile(amount, total, bound, slope):
    loads = [(1 << 20) // math.isqrt(standing ** slope) + 1 for standing in range(2, amount + 1)]
    spare, counts = total - bound - (amount - 1), [1] * (amount - 1)
    while spare > 0:
        movable = [i for i in range(amount - 1) if counts[i] < bound]
        mass, left = sum([loads[i] for i in movable]), spare
        for i in movable:
            more = min(bound - counts[i], max(1, left * loads[i] // mass), spare)
            counts[i] = counts[i] + more
            spare = spare - more
    return np.array([bound] + counts)


def uneven(own_key, count, total, limit, lean):
    if count == 2:
        one = jax.random.randint(own_key, (), max(1, total - limit), min(limit, total - 1) + 1)
        return jnp.stack([one, total - one])
    tallies = jnp.asarray(profile(count, total, limit, lean), jnp.int32)
    twos = (count - 1) // 2
    giver, receiver = tallies[1:1 + 2 * twos:2], tallies[2:2 + 2 * twos:2]
    margin = jnp.minimum(giver - 1, limit - receiver)
    passed = jax.random.randint(jax.random.fold_in(own_key, 1), (twos,), 0, 1 << 20) % (margin + 1)
    tallies = tallies.at[1:1 + 2 * twos:2].set(giver - passed).at[2:2 + 2 * twos:2].set(receiver + passed)
    return tallies[jax.random.permutation(jax.random.fold_in(own_key, 2), count)]


def routed_block(key, own, number, rows, amount, top, limit, slope):
    sequence = jax.random.permutation(key, amount)
    crowded, common = load_shares(amount, rows * top, limit, slope, True), load_shares(amount, rows * top, limit, slope, False)
    places = jnp.arange(amount)

    def named(sizes, rotation):
        used = int((sizes > 0).sum())
        fixed = max(1, used // 4)
        shifted = fixed + (places - fixed + rotation * (used - fixed)) % max(1, amount - fixed)
        return jnp.zeros((amount,), jnp.int32).at[sequence[jnp.where(places < fixed, places, shifted)]].set(jnp.asarray(sizes, jnp.int32))

    sizes = jnp.where(number % 4 == 0, named(crowded, number // 4), named(common, number - number // 4 - 1))
    mixed = jax.random.permutation(jax.random.fold_in(own, 3), amount)
    source_of, taker = mixed[0:amount // 2 * 2:2], mixed[1:amount // 2 * 2:2]
    slack = jnp.minimum(sizes[source_of] - 1, limit - sizes[taker]) // 2
    slack = jnp.where((source_of == sequence[0]) | (taker == sequence[0]) | (sizes[taker] == 0), 0, jnp.maximum(slack, 0))
    shifted = jax.random.randint(jax.random.fold_in(own, 4), (amount // 2,), 0, 1 << 20) % (slack + 1)
    sizes = sizes.at[source_of].add(-shifted).at[taker].add(shifted)
    items = jnp.searchsorted(jnp.cumsum(sizes), jnp.arange(rows * top), side="right").astype(jnp.int32)
    grid = items.reshape(top, rows).T
    grid = grid[jax.random.permutation(jax.random.fold_in(own, 1), rows)]
    rotation = jax.random.randint(jax.random.fold_in(own, 2), (rows, 1), 0, top)
    return jnp.take_along_axis(grid, (jnp.arange(top)[None, :] + rotation) % top, axis=1)


def load_shares(number_of, total, reach, lean, full):
    loads = [(1 << 20) // math.isqrt(rank ** lean) + 1 for rank in range(1, number_of + 1)]
    largest = reach if full else min(reach, max(-(-total // number_of), total * loads[0] // sum(loads)))
    least = 1 if total - largest >= number_of - 1 else 0
    given, spare = [largest] + [least] * (number_of - 1), total - largest - least * (number_of - 1)
    while spare > 0:
        movable = [i for i in range(1, number_of) if given[i] < largest] or [i for i in range(1, number_of) if given[i] < reach]
        whole, left = sum([loads[i] for i in movable]), spare
        for i in movable:
            addition = min(reach - given[i], max(1, left * loads[i] // whole), spare)
            given[i] = given[i] + addition
            spare = spare - addition
    return np.array(given)


def scatter_about(own_key, dims, deviation, most, pieces=(), held_as=jnp.bfloat16):
    values = jax.random.normal(own_key, dims, jnp.float32) * deviation
    if len(pieces) > 0:
        values = block_levels(own_key, dims, pieces, -0.22, 0.18) * values
    return jnp.clip(values, min=-most, max=most).astype(held_as)


def setup_inputs(seed: int = 0) -> dict:
    keys = jax.random.split(jax.random.key(seed), 9)
    tetrahedron_defect_values = scatter_about(keys[0], (TETS,), 1.0, 6.0, ((0, 128),), jnp.float32)
    tetrahedron_destination_block_keys = jax.random.split(jax.random.fold_in(keys[1], 1), TETS // TET_DEV)
    tetrahedron_destination_block_turns = jax.random.permutation(jax.random.fold_in(keys[1], 3), TETS // TET_DEV)
    tetrahedron_destination_block = jax.vmap(lambda own, number: routed_block(jax.random.fold_in(keys[1], 2), own, number, TET_DEV, DEVICES, 1, CAP, 2))(tetrahedron_destination_block_keys, tetrahedron_destination_block_turns).reshape((TETS, 1))
    active_entries_per_part = uneven(keys[2], DEVICES, DEVICES * TET_DEV * 3 // 4, TET_DEV, 2).astype(jnp.int32)
    corner_factor_block_index = touch_ends(jax.random.randint(keys[3], (4, SLOTS), 0, CX * CY), jax.random.fold_in(keys[3], 1), 0, (CX * CY) - 1).astype(jnp.int32)
    corner_factor_elevation = touch_ends(jax.random.randint(keys[4], (4, SLOTS), 0, SPAN_ALONG_Z), jax.random.fold_in(keys[4], 1), 0, SPAN_ALONG_Z - 1).astype(jnp.int32)
    corner_interpolation_factors = jnp.clip(0.1 + 0.9 * jax.random.uniform(keys[5], (4, SLOTS), jnp.float32) ** block_levels(keys[5], (4, SLOTS), ((1, 128),), -0.2, 0.2), 0.1, 1.0)
    baseline_heat_coefficient = jnp.clip(jnp.exp(math.log(5.0) - 2.3025851 * jax.random.uniform(keys[6], (SPAN_ALONG_X, SPAN_ALONG_Y, SPAN_ALONG_Z), jnp.float32) ** block_levels(keys[6], (SPAN_ALONG_X, SPAN_ALONG_Y, SPAN_ALONG_Z), ((0, 8), (1, 16)), -0.2, 0.2)), 0.5, 5.0)
    thermal_state_iterate = scatter_about(keys[7], (SPAN_ALONG_X, SPAN_ALONG_Y, SPAN_ALONG_Z), 1.0, 3.0, ((0, 8), (1, 16)), jnp.float32)
    return {"tetrahedron_defect_values": tetrahedron_defect_values, "tetrahedron_destination_block": tetrahedron_destination_block, "active_entries_per_part": active_entries_per_part, "corner_factor_block_index": corner_factor_block_index, "corner_factor_elevation": corner_factor_elevation, "corner_interpolation_factors": corner_interpolation_factors, "baseline_heat_coefficient": baseline_heat_coefficient, "thermal_state_iterate": thermal_state_iterate}


damping_rate = 0.05
relax_weight = 0.6
link_scale = 1.0 / 52.0
neighbours = [(a, b, c) for a in (-1, 0, 1) for b in (-1, 0, 1) for c in (-1, 0, 1) if (a, b, c) != (0, 0, 0)]


def nearby(x, a, b, c, shape_now):
    return x[1 + a:1 + a + shape_now[0], 1 + b:1 + b + shape_now[1], 1 + c:1 + c + shape_now[2]]


def operate(field, heat_flux_operator, field_wide, conduct_wide):
    accum = damping_rate * heat_flux_operator * field
    for a, b, c in neighbours:
        accum = accum + link_scale * (heat_flux_operator + nearby(conduct_wide, a, b, c, field.shape)) * (field - nearby(field_wide, a, b, c, field.shape))
    return accum


def diagonal_of(heat_flux_operator, conduct_wide):
    accum = damping_rate * heat_flux_operator
    for a, b, c in neighbours:
        accum = accum + link_scale * (heat_flux_operator + nearby(conduct_wide, a, b, c, heat_flux_operator.shape))
    return accum


def restrict(x):
    s = x.shape
    return 0.5 * jnp.sum(x.reshape(s[0] // 2, 2, s[1] // 2, 2, s[2] // 2, 2), axis=(1, 3, 5))


def coarsen(x):
    s = x.shape
    return 0.125 * jnp.sum(x.reshape(s[0] // 2, 2, s[1] // 2, 2, s[2] // 2, 2), axis=(1, 3, 5))


def prolong(x):
    return jnp.repeat(jnp.repeat(jnp.repeat(x, 2, axis=0), 2, axis=1), 2, axis=2)


def relax(error_now, source_term, heat_flux_operator, conduct_wide, diag_term, widen):
    return error_now + relax_weight * (source_term - operate(error_now, heat_flux_operator, widen(error_now), conduct_wide)) / diag_term


def widen_all(x):
    return jnp.pad(x, 1)


def solve_whole(source_term, heat_flux_operator):
    kappa_wide = jnp.pad(heat_flux_operator, 1)
    diag_term = diagonal_of(heat_flux_operator, kappa_wide)
    error_now = relax_weight * source_term / diag_term
    for j in range(CSWEEPS - 1):
        error_now = relax(error_now, source_term, heat_flux_operator, kappa_wide, diag_term, widen_all)
    return error_now


def vcycle(source_term, heat_flux_operator, widen_field, widen_kappa, coarse_solve):
    kappas = [heat_flux_operator]
    for i in range(LEVELS):
        kappas.append(coarsen(kappas[-1]))
    saved = []
    for i in range(LEVELS):
        kappa_wide = widen_kappa(kappas[i])
        diag_term = diagonal_of(kappas[i], kappa_wide)
        error_now = relax_weight * source_term / diag_term
        for j in range(NU - 1):
            error_now = relax(error_now, source_term, kappas[i], kappa_wide, diag_term, widen_field)
        leftover = source_term - operate(error_now, kappas[i], widen_field(error_now), kappa_wide)
        saved.append((error_now, source_term, kappa_wide, diag_term))
        source_term = restrict(leftover)
    error_now = coarse_solve(source_term, kappas[LEVELS])
    for i in reversed(range(LEVELS)):
        fine_error, fine_source, kappa_wide, diag_term = saved[i]
        error_now = fine_error + prolong(error_now)
        for j in range(NU):
            error_now = relax(error_now, fine_source, kappas[i], kappa_wide, diag_term, widen_field)
    return error_now


def reference(tetrahedron_defect_values, tetrahedron_destination_block, active_entries_per_part, corner_factor_block_index, corner_factor_elevation, corner_interpolation_factors, baseline_heat_coefficient, thermal_state_iterate):
    devices = N_BX * N_BY
    brick_slots = devices * CAP
    target_brick = tetrahedron_destination_block[:, 0].reshape(devices, TET_DEV)
    residual_rows = tetrahedron_defect_values.reshape(devices, TET_DEV)
    positions = jnp.arange(TET_DEV, dtype=jnp.int32)
    brick_ids = jnp.arange(devices, dtype=jnp.int32)

    def ranks(packed):
        target_row, count = packed
        is_live = positions < count
        one_hot = ((target_row[:, None] == brick_ids[None, :]) & is_live[:, None]).astype(jnp.int32)
        running = jnp.cumsum(one_hot, axis=0)
        return jnp.sum(one_hot * running, axis=1) - 1

    slot_rank = lax.map(ranks, (target_brick, active_entries_per_part))
    is_live = positions[None, :] < active_entries_per_part[:, None]
    source = jnp.arange(devices, dtype=jnp.int32)[:, None]
    slot = target_brick * brick_slots + source * CAP + slot_rank
    slot = jnp.where(is_live, slot, SLOTS).astype(jnp.int32)
    slot_values = jnp.zeros((SLOTS,), jnp.float32).at[slot.reshape(-1)].set(residual_rows.reshape(-1), mode="drop")
    brick = jnp.arange(SLOTS, dtype=jnp.int32) // brick_slots
    brick_row = (brick // N_BY)[None, :]
    brick_col = (brick % N_BY)[None, :]
    cell_x = brick_row * CX + corner_factor_block_index // CY
    cell_y = brick_col * CY + corner_factor_block_index % CY
    cell_z = corner_factor_elevation
    flat_cells = ((cell_x * SPAN_ALONG_Y + cell_y) * SPAN_ALONG_Z + cell_z).astype(jnp.int32)
    deposits = (corner_interpolation_factors * slot_values[None, :]).reshape(-1)
    rhs = jnp.zeros((SPAN_ALONG_X * SPAN_ALONG_Y * SPAN_ALONG_Z,), jnp.float32).at[flat_cells.reshape(-1)].add(deposits).reshape(SPAN_ALONG_X, SPAN_ALONG_Y, SPAN_ALONG_Z)
    heat_flux_operator = baseline_heat_coefficient * jnp.exp(0.4 * thermal_state_iterate)
    grid_correction = vcycle(rhs, heat_flux_operator, widen_all, widen_all, solve_whole)
    read_back = jnp.sum(corner_interpolation_factors * grid_correction.reshape(-1)[flat_cells], axis=0)
    picked = read_back[jnp.where(is_live, slot, 0).astype(jnp.int32)]
    tet_correction = jnp.where(is_live, picked, jnp.zeros_like(picked))
    return grid_correction, tet_correction.reshape(-1)
```

```python
import functools

import jax
import jax.numpy as jnp
from jax import lax
from jax.experimental import pallas as pl
from jax.experimental.pallas import tpu as pltpu
from jax.sharding import PartitionSpec as P

NX, NY = 8, 16
DEVICES = NX * NY
CAP = 96
ROWS = 8192
SLOTS = DEVICES * CAP
F32 = jnp.float32
BF16 = jnp.bfloat16
VMEM_BYTES = 56 * 1024 * 1024


def iota(shape, dim):
    return lax.broadcasted_iota(jnp.int32, shape, dim)


def pieces(x, count):
    parts = []
    for _ in range(count):
        part = x.astype(BF16)
        parts.append(part)
        x = x - part.astype(F32)
    return parts


def dot(a, b):
    return jnp.dot(a, b, preferred_element_type=F32)


def dot_nt(a, b):
    return lax.dot_general(a, b, (((1,), (1,)), ((), ())), preferred_element_type=F32)


def split_dot(x, m, count=3):
    return sum(dot(p, m) for p in pieces(x, count))


def dot_split(m, x, count=3):
    return sum(dot(m, p) for p in pieces(x, count))


def as_bf16(mask):
    return jnp.where(mask, 1.0, 0.0).astype(BF16)


def pair_rows(coarse, fine):
    return as_bf16(iota((coarse, fine), 1) // 2 == iota((coarse, fine), 0))


def pair_lanes(fine, coarse, at=0):
    return as_bf16(iota((fine, coarse), 0) // 2 + at == iota((fine, coarse), 1))


def rank_kernel(active_ref, dest_ref, value_ref, out_ref, rank_ref, run_ref, acc_ref):
    active = active_ref[0]
    wide = 256
    upper = as_bf16(iota((wide, wide), 0) < iota((wide, wide), 1))
    ones = jnp.ones((wide, wide), BF16)
    bricks = iota((DEVICES, wide), 0)
    ranks = iota((CAP, wide), 0)
    run_ref[...] = jnp.zeros_like(run_ref)
    acc_ref[...] = jnp.zeros_like(acc_ref)

    def step(i, carry):
        def row(ref):
            return jnp.concatenate([ref[pl.ds(2 * i, 1), :], ref[pl.ds(2 * i + 1, 1), :]], axis=1)

        live = i * wide + iota((1, wide), 1) < active
        dest = jnp.where(live, row(dest_ref), -1)
        hot = jnp.where(bricks == dest, 1.0, 0.0)
        hot16 = hot.astype(BF16)
        run = run_ref[...]
        rank = jnp.sum(hot * (dot(hot16, upper) + run), axis=0, keepdims=True).astype(jnp.int32)
        run_ref[...] = run + dot(hot16, ones)
        rank_ref[pl.ds(2 * i, 1), :] = rank[:, :128]
        rank_ref[pl.ds(2 * i + 1, 1), :] = rank[:, 128:]
        value = row(value_ref)
        at = ranks == rank
        total = acc_ref[...]
        for part in pieces(value, 3):
            total = total + dot_nt(hot16, jnp.where(at, part.astype(F32), 0.0).astype(BF16))
        acc_ref[...] = total
        return carry

    lax.fori_loop(0, ROWS // wide, step, 0)
    out_ref[...] = acc_ref[...]


def pick_kernel(active_ref, dest_ref, rank_ref, back_ref, out_ref):
    active = active_ref[0]
    wide = 256
    bricks = iota((DEVICES, wide), 0)
    ranks = iota((CAP, wide), 0)
    table = jnp.transpose(back_ref[...])
    parts = pieces(table, 3)

    def step(i, carry):
        def row(ref):
            return jnp.concatenate([ref[pl.ds(2 * i, 1), :], ref[pl.ds(2 * i + 1, 1), :]], axis=1)

        live = i * wide + iota((1, wide), 1) < active
        dest = jnp.where(live, row(dest_ref), -1)
        hot16 = as_bf16(bricks == dest)
        columns = dot(parts[0], hot16) + dot(parts[1], hot16) + dot(parts[2], hot16)
        picked = jnp.sum(jnp.where(ranks == row(rank_ref), columns, 0.0), axis=0, keepdims=True)
        out_ref[pl.ds(2 * i, 1), :] = picked[:, :128]
        out_ref[pl.ds(2 * i + 1, 1), :] = picked[:, 128:]
        return carry

    lax.fori_loop(0, ROWS // wide, step, 0)


CHUNK = 1024


def deposit_kernel(value_ref, column_ref, depth_ref, factor_ref, rhs_ref, low_ref, high_ref, acc_ref):
    acc_ref[...] = jnp.zeros_like(acc_ref)
    columns = iota((512, CHUNK), 0)
    depths = iota((256, CHUNK), 0)

    def step(i, carry):
        at = pl.ds(pl.multiple_of(i * CHUNK, CHUNK), CHUNK)
        value = value_ref[:, at]
        total = acc_ref[...]
        for k in range(4):
            amount = factor_ref[k : k + 1, at] * value
            hi = amount.astype(BF16).astype(F32)
            lo = amount - hi
            hot = as_bf16(columns == column_ref[k : k + 1, at])
            here = depths == depth_ref[k : k + 1, at]
            spread = jnp.concatenate(
                [jnp.where(here, hi, 0.0).astype(BF16), jnp.where(here, lo, 0.0).astype(BF16)], axis=0
            )
            total = total + dot_nt(hot, spread)
        acc_ref[...] = total
        return carry

    lax.fori_loop(0, SLOTS // CHUNK, step, 0)
    rhs = (acc_ref[:, :256] + acc_ref[:, 256:]).reshape(16, 32, 256)
    rhs_ref[...] = rhs
    low_ref[...] = rhs[:, :8]
    high_ref[...] = rhs[:, 24:]


def box(v, z, depth, rows=None):
    n, m = v.shape
    v = (
        v
        + jnp.where(z == 0, 0.0, pltpu.roll(v, 1, axis=1))
        + jnp.where(z == depth - 1, 0.0, pltpu.roll(v, m - 1, axis=1))
    )
    up, down = pltpu.roll(v, 1, axis=0), pltpu.roll(v, n - 1, axis=0)
    if rows is not None:
        up = jnp.where(rows == 0, 0.0, up)
        down = jnp.where(rows == n - 1, 0.0, down)
    return v + up + down


def near(ref, x):
    return ref[x - 1] + ref[x] + ref[x + 1]


def flow(e, c, q, x, boxed):
    return q[x] * boxed(near(e, x)) + boxed(near(c, x)) - 2.0 * c[x]


def set_weights(q, w, diag, lo, hi, boxed):
    def body(x, carry):
        here = q[x]
        d = 27.6 * here + boxed(near(q, x))
        w[x] = jnp.where(here > 0.0, 0.6 / d, 0.0)
        if diag is not None:
            diag[x] = d
        return carry

    lax.fori_loop(lo, hi, body, 0)


def first_guess(e, c, q, w, r, lo, hi):
    def body(x, carry):
        first = w[x] * r[x]
        e[x] = first
        c[x] = q[x] * first
        return carry

    lax.fori_loop(lo, hi, body, 0)


def sweep(e, c, e2, c2, q, w, r, lo, hi, boxed):
    def body(x, carry):
        new = 0.4 * e[x] + w[x] * (r[x] + flow(e, c, q, x, boxed))
        e2[x] = new
        if c2 is not None:
            c2[x] = q[x] * new
        return carry

    lax.fori_loop(lo, hi, body, 0)


def pack_two(pairs):
    both = dot_split(pair_rows(32, 64), pairs.reshape(64, 128))
    return split_dot(both[:16], pair_lanes(128, 128)) + split_dot(both[16:], pair_lanes(128, 128, 64))


def halve(pairs):
    thin = split_dot(pairs.reshape(256, 256), pair_lanes(256, 128))
    return dot_split(pair_rows(128, 256), thin)


def kappa_kernel(base_ref, state_ref, q_ref, q1_ref, low_ref, high_ref, q2_ref):
    q = base_ref[...] * jnp.exp(0.4 * state_ref[...]) * (1.0 / 52.0)
    q_ref[...] = q
    q1 = 0.125 * halve(jnp.sum(q.reshape(8, 2, 32, 256), axis=1)).reshape(8, 16, 128)
    packed = jnp.concatenate([q1[:4], q1[4:]], axis=2)
    q1_ref[...] = packed
    low_ref[0:16] = q[:, :8]
    high_ref[0:16] = q[:, 24:]
    low_ref[16:20] = packed[:, :8]
    high_ref[16:20] = packed[:, 8:]
    q2_ref[...] = 0.125 * pack_two(jnp.sum(q1.reshape(4, 2, 16, 128), axis=1))


def down_kernel(
    q_own, q_ylo, q_yhi, q_xlo, q_xhi, r_own, r_ylo, r_yhi, r_xlo, r_xhi,
    q, w, r, e, r1_ref, low_ref, high_ref,
    c, e2, c2, diag, pairs,
):
    z = iota((48, 256), 1)
    boxed = functools.partial(box, z=z, depth=256)
    q[0:6] = q_xlo[0:6]
    q[22:28] = q_xhi[0:6]
    q[6:22, 0:8] = q_ylo[0:16]
    q[6:22, 8:40] = q_own[...]
    q[6:22, 40:48] = q_yhi[0:16]
    r[1:6] = r_xlo[...]
    r[22:27] = r_xhi[...]
    r[6:22, 0:8] = r_ylo[...]
    r[6:22, 8:40] = r_own[...]
    r[6:22, 40:48] = r_yhi[...]
    set_weights(q, w, diag, 1, 27, boxed)
    first_guess(e, c, q, w, r, 1, 27)
    sweep(e, c, e2, c2, q, w, r, 2, 26, boxed)
    sweep(e2, c2, e, c, q, w, r, 3, 25, boxed)

    def left(x):
        return (r[x] + flow(e, c, q, x, boxed) - diag[x] * e[x])[8:40]

    def body(i, carry):
        pairs[i] = left(6 + 2 * i) + left(7 + 2 * i)
        return carry

    lax.fori_loop(0, 8, body, 0)
    r1 = 0.5 * halve(pairs[...]).reshape(8, 16, 128)
    r1_ref[...] = r1
    low_ref[...] = r1[:, :8]
    high_ref[...] = r1[:, 8:]


def unpack_one(packed):
    return jnp.concatenate([packed[..., :128], packed[..., 128:]], axis=0)


def down_one_kernel(
    q_own, q_ylo, q_yhi, q_xlo, q_xhi, r_cat, r_xlo, r_xhi,
    q, w, r, e, out_ref,
    c, e2, c2, diag, pairs,
):
    z = iota((32, 128), 1)
    boxed = functools.partial(box, z=z, depth=128)
    q[0:8] = unpack_one(q_xlo[6:10, 0:32])
    q[16:24] = unpack_one(q_xhi[6:10, 0:32])
    q[8:16, 0:8] = unpack_one(q_ylo[16:20])
    q[8:16, 8:24] = unpack_one(q_own[...])
    q[8:16, 24:32] = unpack_one(q_yhi[16:20])
    r[0:8] = r_xlo[...]
    r[8:16] = r_cat[...]
    r[16:24] = r_xhi[...]
    set_weights(q, w, diag, 1, 23, boxed)
    first_guess(e, c, q, w, r, 1, 23)
    sweep(e, c, e2, c2, q, w, r, 2, 22, boxed)
    sweep(e2, c2, e, c, q, w, r, 3, 21, boxed)

    def left(x):
        return (r[x] + flow(e, c, q, x, boxed) - diag[x] * e[x])[8:24]

    def body(i, carry):
        pairs[i] = left(8 + 2 * i) + left(9 + 2 * i)
        return carry

    lax.fori_loop(0, 4, body, 0)
    r2 = 0.5 * pack_two(pairs[...])
    out_ref[...] = jnp.broadcast_to(r2[None], (DEVICES, 16, 128))


def ghosts(ref, count, group):
    lane = iota(ref.shape[1:], 1)
    ref[0] = jnp.where(lane >= group, pltpu.roll(ref[count], group, axis=1), 0.0)
    ref[count + 1] = jnp.where(lane < 128 - group, pltpu.roll(ref[1], 128 - group, axis=1), 0.0)


def assemble_two(gathered, ref):
    lane = iota((8, 128), 1)
    for bx in range(4):
        for by in range(NY):
            for j in range(2):
                a = gathered[bx * NY + by, j * 8 : j * 8 + 8]
                b = gathered[(bx + 4) * NY + by, j * 8 : j * 8 + 8]
                rows = slice(by * 8, by * 8 + 8)
                ref[1 + bx * 4 + j, rows] = jnp.where(lane < 64, a, pltpu.roll(b, 64, axis=1))
                ref[1 + bx * 4 + 2 + j, rows] = jnp.where(lane < 64, pltpu.roll(a, 64, axis=1), b)


def up_kernel(
    place_ref, r2_all, q2_all, q1, w1, r1, e1, q0, w0, r0, e0,
    column_ref, depth_ref, factor_ref,
    grid_ref, back_ref,
    q2, w2, d2, r2, a2, ca2, b2, cb2,
    q3, w3, r3, a3, ca3, b3, cb3,
    last2, s1, c1, t1, ct1, s0, c0, t0, ct0, hi_ref, lo_ref,
):
    bx, by = place_ref[0], place_ref[1]
    z2 = iota((128, 128), 1) % 64
    rows2 = iota((128, 128), 0)
    boxed2 = functools.partial(box, z=z2, depth=64, rows=rows2)
    assemble_two(q2_all, q2)
    assemble_two(r2_all, r2)
    ghosts(q2, 16, 64)
    set_weights(q2, w2, d2, 1, 17, boxed2)
    first_guess(a2, ca2, q2, w2, r2, 1, 17)

    def sweep2(e, c, e_to, c_to):
        ghosts(e, 16, 64)
        ghosts(c, 16, 64)
        sweep(e, c, e_to, c_to, q2, w2, r2, 1, 17, boxed2)

    sweep2(a2, ca2, b2, cb2)
    sweep2(b2, cb2, a2, ca2)
    ghosts(a2, 16, 64)
    ghosts(ca2, 16, 64)
    lanes_low, lanes_high = pair_lanes(128, 128), None
    src, dst = iota((128, 128), 0), iota((128, 128), 1)
    lane_maps = [as_bf16(src // 64 * 64 + at + src % 64 // 2 == dst) for at in (0, 32)]
    rows_half = pair_rows(64, 128)

    def left(x):
        return r2[x] + flow(a2, ca2, q2, x, boxed2) - d2[x] * a2[x]

    def coarse_plane(low, high):
        return dot_split(rows_half, split_dot(low, lane_maps[0]) + split_dot(high, lane_maps[1]))

    for x in range(4):
        r3[1 + x] = 0.5 * coarse_plane(
            left(1 + 2 * x) + left(2 + 2 * x), left(9 + 2 * x) + left(10 + 2 * x)
        )
        q3[1 + x] = 0.125 * coarse_plane(
            q2[1 + 2 * x] + q2[2 + 2 * x], q2[9 + 2 * x] + q2[10 + 2 * x]
        )
    z3 = iota((64, 128), 1) % 32
    rows3 = iota((64, 128), 0)
    boxed3 = functools.partial(box, z=z3, depth=32, rows=rows3)
    ghosts(q3, 4, 32)
    set_weights(q3, w3, None, 1, 5, boxed3)
    first_guess(a3, ca3, q3, w3, r3, 1, 5)
    now, later = (a3, ca3), (b3, cb3)
    for _ in range(7):
        ghosts(now[0], 4, 32)
        ghosts(now[1], 4, 32)
        sweep(*now, *later, q3, w3, r3, 1, 5, boxed3)
        now, later = later, now
    e3 = now[0]
    src, dst = iota((128, 128), 1), iota((128, 128), 0)
    lane_back = [as_bf16(src // 64 * 64 + at + src % 64 // 2 == dst) for at in (0, 32)]
    rows_double = as_bf16(iota((128, 64), 0) // 2 == iota((128, 64), 1))
    for x in range(8):
        more = dot_split(rows_double, split_dot(e3[1 + x % 4], lane_back[x // 4]))
        for j in (1 + 2 * x, 2 + 2 * x):
            new = a2[j] + more
            a2[j] = new
            ca2[j] = q2[j] * new
    sweep2(a2, ca2, b2, cb2)
    sweep2(b2, cb2, a2, ca2)
    ghosts(a2, 16, 64)
    ghosts(ca2, 16, 64)
    last2[:, 0:8] = jnp.zeros((16, 8, 128), F32)
    last2[:, 136:144] = jnp.zeros((16, 8, 128), F32)

    def final2(x, carry):
        last2[x - 1, 8:136] = 0.4 * a2[x] + w2[x] * (r2[x] + flow(a2, ca2, q2, x, boxed2))
        return carry

    lax.fori_loop(1, 17, final2, 0)
    z1 = iota((32, 128), 1)
    boxed1 = functools.partial(box, z=z1, depth=128)
    widen_lanes = as_bf16(iota((128, 128), 1) // 2 == iota((128, 128), 0))
    widen_rows = as_bf16((iota((32, 24), 0) + 8) // 2 == iota((32, 24), 1))
    for j in range(10):
        x = bx * 4 - 3 + j
        inside = jnp.logical_and(x >= 0, x < 32)
        at = jnp.clip(x, 0, 31)
        window = last2[lax.rem(at, 16), pl.ds(pl.multiple_of(by * 8, 8), 24), :]
        window = jnp.where(at >= 16, pltpu.roll(window, 64, axis=1), window)
        window = jnp.where(inside, window, 0.0)
        more = dot_split(widen_rows, split_dot(window, widen_lanes))
        for p in (2 * j + 2, 2 * j + 3):
            if 3 <= p < 21:
                new = e1[p] + more
                s1[p] = new
                c1[p] = q1[p] * new
    sweep(s1, c1, t1, ct1, q1, w1, r1, 4, 20, boxed1)
    sweep(t1, ct1, s1, c1, q1, w1, r1, 5, 19, boxed1)
    sweep(s1, c1, t1, None, q1, w1, r1, 6, 18, boxed1)
    z0 = iota((48, 256), 1)
    boxed0 = functools.partial(box, z=z0, depth=256)
    wide_lanes = as_bf16(iota((128, 256), 1) // 2 == iota((128, 256), 0))
    wide_rows = as_bf16((iota((48, 32), 0) + 8) // 2 == iota((48, 32), 1))

    def widen(j, carry):
        more = dot_split(wide_rows, split_dot(t1[6 + j], wide_lanes))
        for p in (2 * j + 2, 2 * j + 3):
            new = e0[p] + more
            s0[p] = new
            c0[p] = q0[p] * new
        return carry

    lax.fori_loop(0, 12, widen, 0)
    sweep(s0, c0, t0, ct0, q0, w0, r0, 4, 24, boxed0)
    sweep(t0, ct0, s0, c0, q0, w0, r0, 5, 23, boxed0)

    def final0(x, carry):
        new = 0.4 * s0[x] + w0[x] * (r0[x] + flow(s0, c0, q0, x, boxed0))
        grid_ref[x - 6] = new[8:40]
        return carry

    lax.fori_loop(6, 22, final0, 0)
    grid = jnp.transpose(grid_ref[...].reshape(512, 256))
    hi, lo = pieces(grid, 2)
    hi_ref[...] = hi
    lo_ref[...] = lo
    columns = iota((512, CHUNK), 0)
    depths = iota((256, CHUNK), 0)

    def step(i, carry):
        at = pl.ds(pl.multiple_of(i * CHUNK, CHUNK), CHUNK)
        total = jnp.zeros((1, CHUNK), F32)
        for k in range(4):
            hot = as_bf16(columns == column_ref[k : k + 1, at])
            found = dot(hi_ref[...], hot) + dot(lo_ref[...], hot)
            here = depths == depth_ref[k : k + 1, at]
            picked = jnp.sum(jnp.where(here, found, 0.0), axis=0, keepdims=True)
            total = total + factor_ref[k : k + 1, at] * picked
        back_ref[:, at] = total
        return carry

    lax.fori_loop(0, SLOTS // CHUNK, step, 0)


def struct(*shape, dtype=F32):
    return jax.ShapeDtypeStruct(shape, dtype)


def call(kernel, outs, *args, smem=0, scratch=()):
    vmem = pl.BlockSpec(memory_space=pltpu.VMEM)
    return pl.pallas_call(
        kernel,
        out_shape=outs,
        in_specs=[pl.BlockSpec(memory_space=pltpu.SMEM)] * smem + [vmem] * (len(args) - smem),
        out_specs=tuple(vmem for _ in outs),
        scratch_shapes=[pltpu.VMEM(s, d) for s, d in scratch],
        compiler_params=pltpu.CompilerParams(vmem_limit_bytes=VMEM_BYTES),
    )(*args)


def swap(to_lower, to_upper, axis, count):
    up = [(i, i + 1) for i in range(count - 1)]
    down = [(j, i) for i, j in up]
    return lax.ppermute(to_upper, axis, up), lax.ppermute(to_lower, axis, down)


def shards(values, dest, active, column, depth, factor, base, state):
    dest = dest.reshape(64, 128)
    outgoing, rank = call(
        rank_kernel,
        (struct(DEVICES, CAP), struct(64, 128, dtype=jnp.int32)),
        active, dest, values.reshape(64, 128),
        smem=1, scratch=(((DEVICES, 256), F32), ((DEVICES, CAP), F32)),
    )
    incoming = lax.all_to_all(outgoing, ("bx", "by"), split_axis=0, concat_axis=0, tiled=True)

    q, q1, q_low, q_high, q2 = call(
        kappa_kernel,
        (struct(16, 32, 256), struct(4, 16, 256), struct(20, 8, 256), struct(20, 8, 256), struct(16, 128)),
        base, state,
    )
    q2_all = lax.all_gather(q2[None], ("bx", "by"), axis=0, tiled=True)
    q_ylo, q_yhi = swap(q_low, q_high, "by", NY)
    q1_cat = jnp.pad(jnp.concatenate([q_ylo[16:], q1, q_yhi[16:]], axis=1), ((0, 0), (0, 16), (0, 0)))

    def faces(lo, own, hi, planes, extra=None):
        cat = jnp.concatenate([lo[planes], own[planes], hi[planes]], axis=1)
        return cat if extra is None else jnp.concatenate([cat, extra], axis=0)

    q_xlo, q_xhi = swap(
        faces(q_ylo, q, q_yhi, slice(0, 6), q1_cat), faces(q_ylo, q, q_yhi, slice(10, 16), q1_cat), "bx", NX
    )

    rhs, r_low, r_high = call(
        deposit_kernel,
        (struct(16, 32, 256), struct(16, 8, 256), struct(16, 8, 256)),
        incoming.reshape(1, SLOTS), column, depth, factor,
        scratch=(((512, 512), F32),),
    )
    r_ylo, r_yhi = swap(r_low, r_high, "by", NY)
    r_xlo, r_xhi = swap(
        faces(r_ylo, rhs, r_yhi, slice(0, 5)), faces(r_ylo, rhs, r_yhi, slice(11, 16)), "bx", NX
    )

    ext0, ext1 = (28, 48, 256), (24, 32, 128)
    q0e, w0e, r0e, e0e, r1, low1, high1 = call(
        down_kernel,
        (struct(*ext0),) * 4 + (struct(8, 16, 128), struct(8, 8, 128), struct(8, 8, 128)),
        q, q_ylo, q_yhi, q_xlo, q_xhi, rhs, r_ylo, r_yhi, r_xlo, r_xhi,
        scratch=((ext0, F32),) * 4 + (((8, 32, 256), F32),),
    )
    r1_ylo, r1_yhi = swap(low1, high1, "by", NY)
    r1_cat = jnp.concatenate([r1_ylo, r1, r1_yhi], axis=1)
    r1_xlo, r1_xhi = swap(r1_cat, r1_cat, "bx", NX)

    q1e, w1e, r1e, e1e, r2_out = call(
        down_one_kernel,
        (struct(*ext1),) * 4 + (struct(DEVICES, 16, 128),),
        q1, q_ylo, q_yhi, q_xlo, q_xhi, r1_cat, r1_xlo, r1_xhi,
        scratch=((ext1, F32),) * 4 + (((4, 16, 128), F32),),
    )
    r2_all = lax.all_to_all(r2_out, ("bx", "by"), split_axis=0, concat_axis=0, tiled=True)

    place = jnp.stack([lax.axis_index("bx"), lax.axis_index("by")]).astype(jnp.int32)
    whole2, whole3 = (18, 128, 128), (6, 64, 128)
    grid, back = call(
        up_kernel,
        (struct(16, 32, 256), struct(1, SLOTS)),
        place, r2_all, q2_all, q1e, w1e, r1e, e1e, q0e, w0e, r0e, e0e, column, depth, factor,
        smem=1,
        scratch=((whole2, F32),) * 8
        + ((whole3, F32),) * 7
        + (((16, 144, 128), F32),)
        + ((ext1, F32),) * 4
        + ((ext0, F32),) * 4
        + (((256, 512), BF16),) * 2,
    )
    returned = lax.all_to_all(
        back.reshape(DEVICES, CAP), ("bx", "by"), split_axis=0, concat_axis=0, tiled=True
    )
    (picked,) = call(pick_kernel, (struct(64, 128),), active, dest, rank, returned, smem=1)
    return grid, picked.reshape(ROWS)


def solution(mesh):
    placed = (
        P(("bx", "by")),
        P(("bx", "by"), None),
        P(("bx", "by")),
        P(None, ("bx", "by")),
        P(None, ("bx", "by")),
        P(None, ("bx", "by")),
        P("bx", "by", None),
        P("bx", "by", None),
    )
    return jax.shard_map(
        shards,
        mesh=mesh,
        in_specs=placed,
        out_specs=(P("bx", "by", None), P(("bx", "by"))),
        check_vma=False,
    )
```

```python
import functools

import jax
import jax.numpy as jnp
from jax import lax
from jax.experimental import pallas as pl
from jax.experimental.pallas import tpu as pltpu
from jax.sharding import PartitionSpec as P

NX, NY = 8, 16
DEVICES = NX * NY
CAP = 96
ROWS = 8192
SLOTS = DEVICES * CAP
F32 = jnp.float32
BF16 = jnp.bfloat16
F8 = jnp.float8_e4m3fn
I16 = jnp.int16
UNROLL = 4
RANK_UNROLL = 16
VMEM_BYTES = 56 * 1024 * 1024


def iota(shape, dim):
    return lax.broadcasted_iota(jnp.int32, shape, dim)


def pieces(x, count):
    parts = []
    for _ in range(count):
        part = x.astype(BF16)
        parts.append(part)
        x = x - part.astype(F32)
    return parts


def dot(a, b):
    return jnp.dot(a, b, preferred_element_type=F32)


def dot_nt(a, b):
    return lax.dot_general(a, b, (((1,), (1,)), ((), ())), preferred_element_type=F32)


def split_dot(x, m, count=3):
    return sum(dot(p, m) for p in pieces(x, count))


def dot_split(m, x, count=3):
    return sum(dot(m, p) for p in pieces(x, count))


def as_bf16(mask):
    return jnp.where(mask, 1.0, 0.0).astype(BF16)


def row16(x):
    return jnp.broadcast_to(x, (16, x.shape[1])).astype(I16)[0:1]


def iota16(shape, dim):
    return iota(shape, dim).astype(I16)


def hot16(rows, row):
    return jnp.where(rows == row, jnp.ones((), BF16), jnp.zeros((), BF16))


def pair_rows(coarse, fine):
    return as_bf16(iota((coarse, fine), 1) // 2 == iota((coarse, fine), 0))


def pair_lanes(fine, coarse, at=0):
    return as_bf16(iota((fine, coarse), 0) // 2 + at == iota((fine, coarse), 1))


def rank_kernel(active_ref, dest_ref, value_ref, out_ref, rank_ref, run_ref, acc_ref):
    active = active_ref[0]
    wide = 256
    upper = as_bf16(iota((wide, wide), 0) < iota((wide, wide), 1))
    ones = jnp.ones((wide, wide), BF16)
    bricks = iota16((DEVICES, wide), 0)
    ranks = iota16((CAP, wide), 0)
    zero = jnp.zeros((), BF16)
    run_ref[...] = jnp.zeros_like(run_ref)
    acc_ref[...] = jnp.zeros_like(acc_ref)

    def step(i, carry):
        def row(ref):
            return jnp.concatenate([ref[pl.ds(2 * i, 1), :], ref[pl.ds(2 * i + 1, 1), :]], axis=1)

        live = i * wide + iota((1, wide), 1) < active
        dest = row16(jnp.where(live, row(dest_ref), -1))
        hot = hot16(bricks, dest)
        run = run_ref[...]
        rank = jnp.sum(hot.astype(F32) * (dot(hot, upper) + run), axis=0, keepdims=True)
        rank = rank.astype(jnp.int32)
        run_ref[...] = run + dot(hot, ones)
        rank_ref[pl.ds(2 * i, 1), :] = rank[:, :128]
        rank_ref[pl.ds(2 * i + 1, 1), :] = rank[:, 128:]
        at = ranks == row16(rank)
        total = acc_ref[...]
        for part in pieces(jnp.broadcast_to(row(value_ref), (16, wide)), 2):
            total = total + dot_nt(hot, jnp.where(at, part[0:1], zero))
        acc_ref[...] = total
        return carry

    lax.fori_loop(0, ROWS // wide, step, 0, unroll=RANK_UNROLL)
    out_ref[...] = acc_ref[...]


def pick_kernel(active_ref, dest_ref, rank_ref, back_ref, out_ref):
    active = active_ref[0]
    wide = 256
    bricks = iota16((DEVICES, wide), 0)
    ranks = iota((CAP, wide), 0)
    table = jnp.transpose(back_ref[...])
    hi, lo = pieces(table, 2)

    def step(i, carry):
        def row(ref):
            return jnp.concatenate([ref[pl.ds(2 * i, 1), :], ref[pl.ds(2 * i + 1, 1), :]], axis=1)

        live = i * wide + iota((1, wide), 1) < active
        hot = hot16(bricks, row16(jnp.where(live, row(dest_ref), -1)))
        columns = dot(hi, hot) + dot(lo, hot)
        picked = jnp.sum(jnp.where(ranks == row(rank_ref), columns, 0.0), axis=0, keepdims=True)
        out_ref[pl.ds(2 * i, 1), :] = picked[:, :128]
        out_ref[pl.ds(2 * i + 1, 1), :] = picked[:, 128:]
        return carry

    lax.fori_loop(0, ROWS // wide, step, 0, unroll=RANK_UNROLL)


CHUNK = 2048
TOP = 32768.0


def scale_of(x):
    largest = jnp.maximum(jnp.max(jnp.abs(x), axis=(0, 1), keepdims=True), 1e-30)
    return TOP / largest, largest * (1.0 / TOP)


def two_parts(x):
    hi = x.astype(BF16)
    return hi, x - hi.astype(F32)


def deposit_kernel(value_ref, column_ref, depth_ref, factor_ref, rhs_ref, low_ref, high_ref, acc_ref):
    up, down = scale_of(value_ref[...])
    acc_ref[...] = jnp.zeros_like(acc_ref)
    columns = iota16((512, CHUNK), 0)
    depths = iota16((256, CHUNK), 0)
    zero = jnp.zeros((), BF16)

    def step(i, carry):
        at = pl.ds(pl.multiple_of(i * CHUNK, CHUNK), CHUNK)
        value = value_ref[:, at] * up
        total = acc_ref[...]
        for k in range(4):
            amount = jnp.broadcast_to(factor_ref[k : k + 1, at] * value, (16, CHUNK))
            hi, lo = two_parts(amount)
            lo = lo.astype(BF16)
            hot = hot16(columns, row16(column_ref[k : k + 1, at]))
            here = depths == row16(depth_ref[k : k + 1, at])
            total = total + dot_nt(hot, jnp.where(here, hi[0:1], zero))
            total = total + dot_nt(hot.astype(F8), jnp.where(here, lo[0:1], zero).astype(F8))
        acc_ref[...] = total
        return carry

    lax.fori_loop(0, SLOTS // CHUNK, step, 0)
    rhs = (acc_ref[...] * down).reshape(16, 32, 256)
    rhs_ref[...] = rhs
    low_ref[...] = rhs[:, :8]
    high_ref[...] = rhs[:, 24:]


def box(v, z, depth, rows=None):
    n, m = v.shape
    v = (
        v
        + jnp.where(z == 0, 0.0, pltpu.roll(v, 1, axis=1))
        + jnp.where(z == depth - 1, 0.0, pltpu.roll(v, m - 1, axis=1))
    )
    up, down = pltpu.roll(v, 1, axis=0), pltpu.roll(v, n - 1, axis=0)
    if rows is not None:
        up = jnp.where(rows == 0, 0.0, up)
        down = jnp.where(rows == n - 1, 0.0, down)
    return v + up + down


def near(ref, x):
    return ref[x - 1] + ref[x] + ref[x + 1]


def flow(e, c, q, x, boxed):
    return q[x] * boxed(near(e, x)) + boxed(near(c, x)) - 2.0 * c[x]


def set_weights(q, w, diag, lo, hi, boxed):
    def body(x, carry):
        here = q[x]
        d = 27.6 * here + boxed(near(q, x))
        w[x] = jnp.where(here > 0.0, 0.6 / d, 0.0)
        if diag is not None:
            diag[x] = d
        return carry

    lax.fori_loop(lo, hi, body, 0, unroll=UNROLL)


def first_guess(e, c, q, w, r, lo, hi):
    def body(x, carry):
        first = w[x] * r[x]
        e[x] = first
        c[x] = q[x] * first
        return carry

    lax.fori_loop(lo, hi, body, 0, unroll=UNROLL)


def sweep(e, c, e2, c2, q, w, r, lo, hi, boxed):
    def body(x, carry):
        new = 0.4 * e[x] + w[x] * (r[x] + flow(e, c, q, x, boxed))
        e2[x] = new
        if c2 is not None:
            c2[x] = q[x] * new
        return carry

    lax.fori_loop(lo, hi, body, 0, unroll=UNROLL)


def pack_two(pairs):
    both = dot_split(pair_rows(32, 64), pairs.reshape(64, 128))
    return split_dot(both[:16], pair_lanes(128, 128)) + split_dot(both[16:], pair_lanes(128, 128, 64))


def halve(pairs):
    thin = split_dot(pairs.reshape(256, 256), pair_lanes(256, 128))
    return dot_split(pair_rows(128, 256), thin)


def kappa_kernel(base_ref, state_ref, q_ref, q1_ref, low_ref, high_ref, q2_ref):
    q = base_ref[...] * jnp.exp(0.4 * state_ref[...]) * (1.0 / 52.0)
    q_ref[...] = q
    q1 = 0.125 * halve(jnp.sum(q.reshape(8, 2, 32, 256), axis=1)).reshape(8, 16, 128)
    packed = jnp.concatenate([q1[:4], q1[4:]], axis=2)
    q1_ref[...] = packed
    low_ref[0:16] = q[:, :8]
    high_ref[0:16] = q[:, 24:]
    low_ref[16:20] = packed[:, :8]
    high_ref[16:20] = packed[:, 8:]
    q2_ref[...] = 0.125 * pack_two(jnp.sum(q1.reshape(4, 2, 16, 128), axis=1))


def down_kernel(
    q_own, q_ylo, q_yhi, q_xlo, q_xhi, r_own, r_ylo, r_yhi, r_xlo, r_xhi,
    q, w, r, e, r1_ref, low_ref, high_ref,
    c, e2, c2, diag, pairs,
):
    z = iota((48, 256), 1)
    boxed = functools.partial(box, z=z, depth=256)
    q[0:6] = q_xlo[0:6]
    q[22:28] = q_xhi[0:6]
    q[6:22, 0:8] = q_ylo[0:16]
    q[6:22, 8:40] = q_own[...]
    q[6:22, 40:48] = q_yhi[0:16]
    r[1:6] = r_xlo[...]
    r[22:27] = r_xhi[...]
    r[6:22, 0:8] = r_ylo[...]
    r[6:22, 8:40] = r_own[...]
    r[6:22, 40:48] = r_yhi[...]
    set_weights(q, w, diag, 1, 27, boxed)
    first_guess(e, c, q, w, r, 1, 27)
    sweep(e, c, e2, c2, q, w, r, 2, 26, boxed)
    sweep(e2, c2, e, c, q, w, r, 3, 25, boxed)

    def left(x):
        return (r[x] + flow(e, c, q, x, boxed) - diag[x] * e[x])[8:40]

    def body(i, carry):
        pairs[i] = left(6 + 2 * i) + left(7 + 2 * i)
        return carry

    lax.fori_loop(0, 8, body, 0, unroll=UNROLL // 2)
    r1 = 0.5 * halve(pairs[...]).reshape(8, 16, 128)
    r1_ref[...] = r1
    low_ref[...] = r1[:, :8]
    high_ref[...] = r1[:, 8:]


def unpack_one(packed):
    return jnp.concatenate([packed[..., :128], packed[..., 128:]], axis=0)


def down_one_kernel(
    q_own, q_ylo, q_yhi, q_xlo, q_xhi, r_cat, r_xlo, r_xhi,
    q, w, r, e, out_ref,
    c, e2, c2, diag, pairs,
):
    z = iota((32, 128), 1)
    boxed = functools.partial(box, z=z, depth=128)
    q[0:8] = unpack_one(q_xlo[6:10, 0:32])
    q[16:24] = unpack_one(q_xhi[6:10, 0:32])
    q[8:16, 0:8] = unpack_one(q_ylo[16:20])
    q[8:16, 8:24] = unpack_one(q_own[...])
    q[8:16, 24:32] = unpack_one(q_yhi[16:20])
    r[0:8] = r_xlo[...]
    r[8:16] = r_cat[...]
    r[16:24] = r_xhi[...]
    set_weights(q, w, diag, 1, 23, boxed)
    first_guess(e, c, q, w, r, 1, 23)
    sweep(e, c, e2, c2, q, w, r, 2, 22, boxed)
    sweep(e2, c2, e, c, q, w, r, 3, 21, boxed)

    def left(x):
        return (r[x] + flow(e, c, q, x, boxed) - diag[x] * e[x])[8:24]

    def body(i, carry):
        pairs[i] = left(8 + 2 * i) + left(9 + 2 * i)
        return carry

    lax.fori_loop(0, 4, body, 0, unroll=UNROLL // 2)
    r2 = 0.5 * pack_two(pairs[...])
    out_ref[...] = jnp.broadcast_to(r2[None], (DEVICES, 16, 128))


def ghosts(ref, count, group):
    lane = iota(ref.shape[1:], 1)
    ref[0] = jnp.where(lane >= group, pltpu.roll(ref[count], group, axis=1), 0.0)
    ref[count + 1] = jnp.where(lane < 128 - group, pltpu.roll(ref[1], 128 - group, axis=1), 0.0)


def assemble_two(gathered, ref):
    lane = iota((8, 128), 1)
    for bx in range(4):
        for by in range(NY):
            for j in range(2):
                a = gathered[bx * NY + by, j * 8 : j * 8 + 8]
                b = gathered[(bx + 4) * NY + by, j * 8 : j * 8 + 8]
                rows = slice(by * 8, by * 8 + 8)
                ref[1 + bx * 4 + j, rows] = jnp.where(lane < 64, a, pltpu.roll(b, 64, axis=1))
                ref[1 + bx * 4 + 2 + j, rows] = jnp.where(lane < 64, pltpu.roll(a, 64, axis=1), b)


def up_kernel(
    place_ref, r2_all, q2_all, q1, w1, r1, e1, q0, w0, r0, e0,
    column_ref, depth_ref, factor_ref,
    grid_ref, back_ref,
    q2, w2, d2, r2, a2, ca2, b2, cb2,
    q3, w3, r3, a3, ca3, b3, cb3,
    last2, s1, c1, t1, ct1, s0, c0, t0, ct0, hi_ref, lo_ref,
):
    bx, by = place_ref[0], place_ref[1]
    z2 = iota((128, 128), 1) % 64
    rows2 = iota((128, 128), 0)
    boxed2 = functools.partial(box, z=z2, depth=64, rows=rows2)
    assemble_two(q2_all, q2)
    assemble_two(r2_all, r2)
    ghosts(q2, 16, 64)
    set_weights(q2, w2, d2, 1, 17, boxed2)
    first_guess(a2, ca2, q2, w2, r2, 1, 17)

    def sweep2(e, c, e_to, c_to):
        ghosts(e, 16, 64)
        ghosts(c, 16, 64)
        sweep(e, c, e_to, c_to, q2, w2, r2, 1, 17, boxed2)

    sweep2(a2, ca2, b2, cb2)
    sweep2(b2, cb2, a2, ca2)
    ghosts(a2, 16, 64)
    ghosts(ca2, 16, 64)
    lanes_low, lanes_high = pair_lanes(128, 128), None
    src, dst = iota((128, 128), 0), iota((128, 128), 1)
    lane_maps = [as_bf16(src // 64 * 64 + at + src % 64 // 2 == dst) for at in (0, 32)]
    rows_half = pair_rows(64, 128)

    def left(x):
        return r2[x] + flow(a2, ca2, q2, x, boxed2) - d2[x] * a2[x]

    def coarse_plane(low, high):
        return dot_split(rows_half, split_dot(low, lane_maps[0]) + split_dot(high, lane_maps[1]))

    for x in range(4):
        r3[1 + x] = 0.5 * coarse_plane(
            left(1 + 2 * x) + left(2 + 2 * x), left(9 + 2 * x) + left(10 + 2 * x)
        )
        q3[1 + x] = 0.125 * coarse_plane(
            q2[1 + 2 * x] + q2[2 + 2 * x], q2[9 + 2 * x] + q2[10 + 2 * x]
        )
    z3 = iota((64, 128), 1) % 32
    rows3 = iota((64, 128), 0)
    boxed3 = functools.partial(box, z=z3, depth=32, rows=rows3)
    ghosts(q3, 4, 32)
    set_weights(q3, w3, None, 1, 5, boxed3)
    first_guess(a3, ca3, q3, w3, r3, 1, 5)
    now, later = (a3, ca3), (b3, cb3)
    for _ in range(7):
        ghosts(now[0], 4, 32)
        ghosts(now[1], 4, 32)
        sweep(*now, *later, q3, w3, r3, 1, 5, boxed3)
        now, later = later, now
    e3 = now[0]
    src, dst = iota((128, 128), 1), iota((128, 128), 0)
    lane_back = [as_bf16(src // 64 * 64 + at + src % 64 // 2 == dst) for at in (0, 32)]
    rows_double = as_bf16(iota((128, 64), 0) // 2 == iota((128, 64), 1))
    for x in range(8):
        more = dot_split(rows_double, split_dot(e3[1 + x % 4], lane_back[x // 4]))
        for j in (1 + 2 * x, 2 + 2 * x):
            new = a2[j] + more
            a2[j] = new
            ca2[j] = q2[j] * new
    sweep2(a2, ca2, b2, cb2)
    sweep2(b2, cb2, a2, ca2)
    ghosts(a2, 16, 64)
    ghosts(ca2, 16, 64)
    last2[:, 0:8] = jnp.zeros((16, 8, 128), F32)
    last2[:, 136:144] = jnp.zeros((16, 8, 128), F32)

    def final2(x, carry):
        last2[x - 1, 8:136] = 0.4 * a2[x] + w2[x] * (r2[x] + flow(a2, ca2, q2, x, boxed2))
        return carry

    lax.fori_loop(1, 17, final2, 0, unroll=UNROLL)
    z1 = iota((32, 128), 1)
    boxed1 = functools.partial(box, z=z1, depth=128)
    widen_lanes = as_bf16(iota((128, 128), 1) // 2 == iota((128, 128), 0))
    widen_rows = as_bf16((iota((32, 24), 0) + 8) // 2 == iota((32, 24), 1))
    for j in range(10):
        x = bx * 4 - 3 + j
        inside = jnp.logical_and(x >= 0, x < 32)
        at = jnp.clip(x, 0, 31)
        window = last2[lax.rem(at, 16), pl.ds(pl.multiple_of(by * 8, 8), 24), :]
        window = jnp.where(at >= 16, pltpu.roll(window, 64, axis=1), window)
        window = jnp.where(inside, window, 0.0)
        more = dot_split(widen_rows, split_dot(window, widen_lanes))
        for p in (2 * j + 2, 2 * j + 3):
            if 3 <= p < 21:
                new = e1[p] + more
                s1[p] = new
                c1[p] = q1[p] * new
    sweep(s1, c1, t1, ct1, q1, w1, r1, 4, 20, boxed1)
    sweep(t1, ct1, s1, c1, q1, w1, r1, 5, 19, boxed1)
    sweep(s1, c1, t1, None, q1, w1, r1, 6, 18, boxed1)
    z0 = iota((48, 256), 1)
    boxed0 = functools.partial(box, z=z0, depth=256)
    wide_lanes = as_bf16(iota((128, 256), 1) // 2 == iota((128, 256), 0))
    wide_rows = as_bf16((iota((48, 32), 0) + 8) // 2 == iota((48, 32), 1))

    def widen(j, carry):
        more = dot_split(wide_rows, split_dot(t1[6 + j], wide_lanes))
        for p in (2 * j + 2, 2 * j + 3):
            new = e0[p] + more
            s0[p] = new
            c0[p] = q0[p] * new
        return carry

    lax.fori_loop(0, 12, widen, 0, unroll=UNROLL)
    sweep(s0, c0, t0, ct0, q0, w0, r0, 4, 24, boxed0)
    sweep(t0, ct0, s0, c0, q0, w0, r0, 5, 23, boxed0)

    def final0(x, carry):
        new = 0.4 * s0[x] + w0[x] * (r0[x] + flow(s0, c0, q0, x, boxed0))
        grid_ref[x - 6] = new[8:40]
        return carry

    lax.fori_loop(6, 22, final0, 0, unroll=UNROLL)
    grid = jnp.transpose(grid_ref[...].reshape(512, 256))
    up, down = scale_of(grid)
    hi, lo = two_parts(grid * up)
    hi_ref[...] = hi
    lo_ref[...] = lo.astype(F8)
    columns = iota16((512, CHUNK), 0)
    depths = iota((256, CHUNK), 0)

    def step(i, carry):
        at = pl.ds(pl.multiple_of(i * CHUNK, CHUNK), CHUNK)
        total = jnp.zeros((1, CHUNK), F32)
        for k in range(4):
            hot = hot16(columns, row16(column_ref[k : k + 1, at]))
            found = dot(hi_ref[...], hot) + dot(lo_ref[...], hot.astype(F8))
            here = depths == depth_ref[k : k + 1, at]
            picked = jnp.sum(jnp.where(here, found, 0.0), axis=0, keepdims=True)
            total = total + factor_ref[k : k + 1, at] * picked
        back_ref[:, at] = total * down
        return carry

    lax.fori_loop(0, SLOTS // CHUNK, step, 0)


def struct(*shape, dtype=F32):
    return jax.ShapeDtypeStruct(shape, dtype)


def call(kernel, outs, *args, smem=0, scratch=()):
    vmem = pl.BlockSpec(memory_space=pltpu.VMEM)
    return pl.pallas_call(
        kernel,
        out_shape=outs,
        in_specs=[pl.BlockSpec(memory_space=pltpu.SMEM)] * smem + [vmem] * (len(args) - smem),
        out_specs=tuple(vmem for _ in outs),
        scratch_shapes=[pltpu.VMEM(s, d) for s, d in scratch],
        compiler_params=pltpu.CompilerParams(vmem_limit_bytes=VMEM_BYTES),
    )(*args)


def swap(to_lower, to_upper, axis, count):
    up = [(i, i + 1) for i in range(count - 1)]
    down = [(j, i) for i, j in up]
    return lax.ppermute(to_upper, axis, up), lax.ppermute(to_lower, axis, down)


def shards(values, dest, active, column, depth, factor, base, state):
    dest = dest.reshape(64, 128)
    outgoing, rank = call(
        rank_kernel,
        (struct(DEVICES, CAP), struct(64, 128, dtype=jnp.int32)),
        active, dest, values.reshape(64, 128),
        smem=1, scratch=(((DEVICES, 256), F32), ((DEVICES, CAP), F32)),
    )
    incoming = lax.all_to_all(outgoing, ("bx", "by"), split_axis=0, concat_axis=0, tiled=True)

    q, q1, q_low, q_high, q2 = call(
        kappa_kernel,
        (struct(16, 32, 256), struct(4, 16, 256), struct(20, 8, 256), struct(20, 8, 256), struct(16, 128)),
        base, state,
    )
    q2_all = lax.all_gather(q2[None], ("bx", "by"), axis=0, tiled=True)
    q_ylo, q_yhi = swap(q_low, q_high, "by", NY)
    q1_cat = jnp.pad(jnp.concatenate([q_ylo[16:], q1, q_yhi[16:]], axis=1), ((0, 0), (0, 16), (0, 0)))

    def faces(lo, own, hi, planes, extra=None):
        cat = jnp.concatenate([lo[planes], own[planes], hi[planes]], axis=1)
        return cat if extra is None else jnp.concatenate([cat, extra], axis=0)

    q_xlo, q_xhi = swap(
        faces(q_ylo, q, q_yhi, slice(0, 6), q1_cat), faces(q_ylo, q, q_yhi, slice(10, 16), q1_cat), "bx", NX
    )

    rhs, r_low, r_high = call(
        deposit_kernel,
        (struct(16, 32, 256), struct(16, 8, 256), struct(16, 8, 256)),
        incoming.reshape(1, SLOTS), column, depth, factor,
        scratch=(((512, 256), F32),),
    )
    r_ylo, r_yhi = swap(r_low, r_high, "by", NY)
    r_xlo, r_xhi = swap(
        faces(r_ylo, rhs, r_yhi, slice(0, 5)), faces(r_ylo, rhs, r_yhi, slice(11, 16)), "bx", NX
    )

    ext0, ext1 = (28, 48, 256), (24, 32, 128)
    q0e, w0e, r0e, e0e, r1, low1, high1 = call(
        down_kernel,
        (struct(*ext0),) * 4 + (struct(8, 16, 128), struct(8, 8, 128), struct(8, 8, 128)),
        q, q_ylo, q_yhi, q_xlo, q_xhi, rhs, r_ylo, r_yhi, r_xlo, r_xhi,
        scratch=((ext0, F32),) * 4 + (((8, 32, 256), F32),),
    )
    r1_ylo, r1_yhi = swap(low1, high1, "by", NY)
    r1_cat = jnp.concatenate([r1_ylo, r1, r1_yhi], axis=1)
    r1_xlo, r1_xhi = swap(r1_cat, r1_cat, "bx", NX)

    q1e, w1e, r1e, e1e, r2_out = call(
        down_one_kernel,
        (struct(*ext1),) * 4 + (struct(DEVICES, 16, 128),),
        q1, q_ylo, q_yhi, q_xlo, q_xhi, r1_cat, r1_xlo, r1_xhi,
        scratch=((ext1, F32),) * 4 + (((4, 16, 128), F32),),
    )
    r2_all = lax.all_to_all(r2_out, ("bx", "by"), split_axis=0, concat_axis=0, tiled=True)

    place = jnp.stack([lax.axis_index("bx"), lax.axis_index("by")]).astype(jnp.int32)
    whole2, whole3 = (18, 128, 128), (6, 64, 128)
    grid, back = call(
        up_kernel,
        (struct(16, 32, 256), struct(1, SLOTS)),
        place, r2_all, q2_all, q1e, w1e, r1e, e1e, q0e, w0e, r0e, e0e, column, depth, factor,
        smem=1,
        scratch=((whole2, F32),) * 8
        + ((whole3, F32),) * 7
        + (((16, 144, 128), F32),)
        + ((ext1, F32),) * 4
        + ((ext0, F32),) * 4
        + (((256, 512), BF16), ((256, 512), F8)),
    )
    returned = lax.all_to_all(
        back.reshape(DEVICES, CAP), ("bx", "by"), split_axis=0, concat_axis=0, tiled=True
    )
    (picked,) = call(pick_kernel, (struct(64, 128),), active, dest, rank, returned, smem=1)
    return grid, picked.reshape(ROWS)


def solution(mesh):
    placed = (
        P(("bx", "by")),
        P(("bx", "by"), None),
        P(("bx", "by")),
        P(None, ("bx", "by")),
        P(None, ("bx", "by")),
        P(None, ("bx", "by")),
        P("bx", "by", None),
        P("bx", "by", None),
    )
    return jax.shard_map(
        shards,
        mesh=mesh,
        in_specs=placed,
        out_specs=(P("bx", "by", None), P(("bx", "by"))),
        check_vma=False,
    )
```

```python
import functools

import jax
import jax.numpy as jnp
from jax import lax
from jax.experimental import pallas as pl
from jax.experimental.pallas import tpu as pltpu
from jax.sharding import PartitionSpec as P

NX, NY = 8, 16
DEVICES = NX * NY
CAP = 96
LANES = 128
ROWS = 8192
SLOTS = DEVICES * CAP
F32 = jnp.float32
BF16 = jnp.bfloat16
F8 = jnp.float8_e4m3fn
I16 = jnp.int16
UNROLL = 4
RANK_UNROLL = 16
VMEM_BYTES = 56 * 1024 * 1024


def iota(shape, dim):
    return lax.broadcasted_iota(jnp.int32, shape, dim)


def pieces(x, count):
    parts = []
    for _ in range(count):
        part = x.astype(BF16)
        parts.append(part)
        x = x - part.astype(F32)
    return parts


def dot(a, b):
    return jnp.dot(a, b, preferred_element_type=F32)


def dot_nt(a, b):
    return lax.dot_general(a, b, (((1,), (1,)), ((), ())), preferred_element_type=F32)


def split_dot(x, m, count=3):
    return sum(dot(p, m) for p in pieces(x, count))


def dot_split(m, x, count=3):
    return sum(dot(m, p) for p in pieces(x, count))


def as_bf16(mask):
    return jnp.where(mask, 1.0, 0.0).astype(BF16)


def row16(x):
    return jnp.broadcast_to(x, (16, x.shape[1])).astype(I16)[0:1]


def iota16(shape, dim):
    return iota(shape, dim).astype(I16)


def hot16(rows, row):
    return jnp.where(rows == row, jnp.ones((), BF16), jnp.zeros((), BF16))


def pair_rows(coarse, fine):
    return as_bf16(iota((coarse, fine), 1) // 2 == iota((coarse, fine), 0))


def pair_lanes(fine, coarse, at=0):
    return as_bf16(iota((fine, coarse), 0) // 2 + at == iota((fine, coarse), 1))


def rank_kernel(active_ref, dest_ref, value_ref, out_ref, rank_ref, run_ref, acc_ref):
    active = active_ref[0]
    wide = 256
    upper = as_bf16(iota((wide, wide), 0) < iota((wide, wide), 1))
    ones = jnp.ones((wide, wide), BF16)
    bricks = iota16((DEVICES, wide), 0)
    ranks = iota16((LANES, wide), 0)
    zero = jnp.zeros((), BF16)
    run_ref[...] = jnp.zeros_like(run_ref)
    acc_ref[...] = jnp.zeros_like(acc_ref)

    def step(i, carry):
        def row(ref):
            return jnp.concatenate([ref[pl.ds(2 * i, 1), :], ref[pl.ds(2 * i + 1, 1), :]], axis=1)

        live = i * wide + iota((1, wide), 1) < active
        dest = row16(jnp.where(live, row(dest_ref), -1))
        hot = hot16(bricks, dest)
        run = run_ref[...]
        rank = jnp.sum(hot.astype(F32) * (dot(hot, upper) + run), axis=0, keepdims=True)
        rank = rank.astype(jnp.int32)
        run_ref[...] = run + dot(hot, ones)
        rank_ref[pl.ds(2 * i, 1), :] = rank[:, :128]
        rank_ref[pl.ds(2 * i + 1, 1), :] = rank[:, 128:]
        at = ranks == row16(rank)
        total = acc_ref[...]
        for part in pieces(jnp.broadcast_to(row(value_ref), (16, wide)), 2):
            total = total + dot_nt(hot, jnp.where(at, part[0:1], zero))
        acc_ref[...] = total
        return carry

    lax.fori_loop(0, ROWS // wide, step, 0, unroll=RANK_UNROLL)
    out_ref[...] = acc_ref[...]


def pick_kernel(active_ref, dest_ref, rank_ref, back_ref, out_ref):
    active = active_ref[0]
    wide = 256
    bricks = iota16((DEVICES, wide), 0)
    ranks = iota((LANES, wide), 0)
    table = jnp.transpose(back_ref[...])
    hi, lo = pieces(table, 2)

    def step(i, carry):
        def row(ref):
            return jnp.concatenate([ref[pl.ds(2 * i, 1), :], ref[pl.ds(2 * i + 1, 1), :]], axis=1)

        live = i * wide + iota((1, wide), 1) < active
        hot = hot16(bricks, row16(jnp.where(live, row(dest_ref), -1)))
        columns = dot(hi, hot) + dot(lo, hot)
        picked = jnp.sum(jnp.where(ranks == row(rank_ref), columns, 0.0), axis=0, keepdims=True)
        out_ref[pl.ds(2 * i, 1), :] = picked[:, :128]
        out_ref[pl.ds(2 * i + 1, 1), :] = picked[:, 128:]
        return carry

    lax.fori_loop(0, ROWS // wide, step, 0, unroll=RANK_UNROLL)


CHUNK = 1536
GROUP = 4 * CAP


def to_groups(ref, out):
    a = [ref[pl.ds(i, 32, stride=4), :] for i in range(4)]
    lane = iota((32, 128), 1)

    def moved(x, by):
        return pltpu.roll(x, by, axis=1)

    out[:, 0:128] = jnp.where(lane < 96, a[0], moved(a[1], 96))
    out[:, 128:256] = jnp.where(lane < 64, moved(a[1], 96), moved(a[2], 64))
    out[:, 256:384] = jnp.where(lane < 32, moved(a[2], 64), moved(a[3], 32))


def from_groups(ref, out):
    t = [ref[:, 128 * i : 128 * i + 128] for i in range(3)]
    lane = iota((32, 128), 1)

    def moved(x, by):
        return pltpu.roll(x, by, axis=1)

    out[pl.ds(0, 32, stride=4), :] = t[0]
    out[pl.ds(1, 32, stride=4), :] = jnp.where(lane < 32, moved(t[0], 32), moved(t[1], 32))
    out[pl.ds(2, 32, stride=4), :] = jnp.where(lane < 64, moved(t[1], 64), moved(t[2], 64))
    out[pl.ds(3, 32, stride=4), :] = moved(t[2], 96)
TOP = 32768.0


def scale_of(x):
    largest = jnp.maximum(jnp.max(jnp.abs(x), axis=(0, 1), keepdims=True), 1e-30)
    return TOP / largest, largest * (1.0 / TOP)


def two_parts(x):
    hi = x.astype(BF16)
    return hi, x - hi.astype(F32)


def depth_lane(depth):
    return (depth & 1) * 128 + (depth >> 1)


def deposit_kernel(slots_ref, column_ref, depth_ref, factor_ref, rhs_ref, low_ref, high_ref, acc_ref, value_ref):
    to_groups(slots_ref, value_ref)
    up, down = scale_of(value_ref[...])
    acc_ref[...] = jnp.zeros_like(acc_ref)
    columns = iota16((512, CHUNK), 0)
    depths = iota16((256, CHUNK), 0)
    zero = jnp.zeros((), BF16)

    def step(i, carry):
        at = pl.ds(pl.multiple_of(i * CHUNK, CHUNK), CHUNK)
        groups = [value_ref[pl.ds(i * (CHUNK // GROUP) + j, 1), :] for j in range(CHUNK // GROUP)]
        value = jnp.concatenate(groups, axis=1) * up
        total = acc_ref[...]
        for k in range(4):
            amount = jnp.broadcast_to(factor_ref[k : k + 1, at] * value, (16, CHUNK))
            hi, lo = two_parts(amount)
            lo = lo.astype(BF16)
            hot = hot16(columns, row16(column_ref[k : k + 1, at]))
            here = depths == row16(depth_lane(depth_ref[k : k + 1, at]))
            total = total + dot_nt(hot, jnp.where(here, hi[0:1], zero))
            total = total + dot_nt(hot.astype(F8), jnp.where(here, lo[0:1], zero).astype(F8))
        acc_ref[...] = total
        return carry

    lax.fori_loop(0, SLOTS // CHUNK, step, 0)
    rhs = (acc_ref[...] * down).reshape(16, 32, 256)
    rhs_ref[...] = rhs
    low_ref[...] = rhs[:, :8]
    high_ref[...] = rhs[:, 24:]


def box(v, z, depth, rows=None):
    n, m = v.shape
    v = (
        v
        + jnp.where(z == 0, 0.0, pltpu.roll(v, 1, axis=1))
        + jnp.where(z == depth - 1, 0.0, pltpu.roll(v, m - 1, axis=1))
    )
    up, down = pltpu.roll(v, 1, axis=0), pltpu.roll(v, n - 1, axis=0)
    if rows is not None:
        up = jnp.where(rows == 0, 0.0, up)
        down = jnp.where(rows == n - 1, 0.0, down)
    return v + up + down


def box_parity(v):
    n = v.shape[0]
    even, odd = v[:, :128], v[:, 128:]
    lane = iota((n, 128), 1)
    both = even + odd
    before = jnp.where(lane == 0, 0.0, pltpu.roll(odd, 1, axis=1))
    after = jnp.where(lane == 127, 0.0, pltpu.roll(even, 127, axis=1))
    v = jnp.concatenate([both + before, both + after], axis=1)
    return v + pltpu.roll(v, 1, axis=0) + pltpu.roll(v, n - 1, axis=0)


def parity(dim):
    z, lane = iota((256, 256), dim), iota((256, 256), 1 - dim)
    return as_bf16(z % 2 * 128 + z // 2 == lane)


def near(ref, x):
    return ref[x - 1] + ref[x] + ref[x + 1]


def flow(e, c, q, x, boxed):
    return q[x] * boxed(near(e, x)) + boxed(near(c, x)) - 2.0 * c[x]


def set_weights(q, w, diag, lo, hi, boxed):
    def body(x, carry):
        here = q[x]
        d = 27.6 * here + boxed(near(q, x))
        w[x] = jnp.where(here > 0.0, 0.6 / d, 0.0)
        if diag is not None:
            diag[x] = d
        return carry

    lax.fori_loop(lo, hi, body, 0, unroll=UNROLL)


def first_guess(e, c, q, w, r, lo, hi):
    def body(x, carry):
        first = w[x] * r[x]
        e[x] = first
        c[x] = q[x] * first
        return carry

    lax.fori_loop(lo, hi, body, 0, unroll=UNROLL)


def sweep(e, c, e2, c2, q, w, r, lo, hi, boxed):
    def body(x, carry):
        new = 0.4 * e[x] + w[x] * (r[x] + flow(e, c, q, x, boxed))
        e2[x] = new
        if c2 is not None:
            c2[x] = q[x] * new
        return carry

    lax.fori_loop(lo, hi, body, 0, unroll=UNROLL)


def pack_two(pairs):
    both = dot_split(pair_rows(32, 64), pairs.reshape(64, 128))
    return split_dot(both[:16], pair_lanes(128, 128)) + split_dot(both[16:], pair_lanes(128, 128, 64))


def halve(pairs):
    flat = pairs.reshape(256, 256)
    return dot_split(pair_rows(128, 256), flat[:, :128] + flat[:, 128:])


def kappa_kernel(base_ref, state_ref, q_ref, q1_ref, low_ref, high_ref, q2_ref):
    q = base_ref[...] * jnp.exp(0.4 * state_ref[...]) * (1.0 / 52.0)
    q = split_dot(q.reshape(512, 256), parity(0)).reshape(16, 32, 256)
    q_ref[...] = q
    q1 = 0.125 * halve(jnp.sum(q.reshape(8, 2, 32, 256), axis=1)).reshape(8, 16, 128)
    packed = jnp.concatenate([q1[:4], q1[4:]], axis=2)
    q1_ref[...] = packed
    low_ref[0:16] = q[:, :8]
    high_ref[0:16] = q[:, 24:]
    low_ref[16:20] = packed[:, :8]
    high_ref[16:20] = packed[:, 8:]
    q2_ref[...] = 0.125 * pack_two(jnp.sum(q1.reshape(4, 2, 16, 128), axis=1))


def down_kernel(
    q_own, q_ylo, q_yhi, r_own, r_ylo, r_yhi, xlo, xhi,
    q, w, r, e, r1_ref, low_ref, high_ref,
    c, e2, c2, diag, pairs,
):
    boxed = box_parity
    q[0:6] = xlo[5:11]
    q[22:28] = xhi[5:11]
    q[6:22, 0:8] = q_ylo[0:16]
    q[6:22, 8:40] = q_own[...]
    q[6:22, 40:48] = q_yhi[0:16]
    r[1:6] = xlo[0:5]
    r[22:27] = xhi[0:5]
    r[6:22, 0:8] = r_ylo[...]
    r[6:22, 8:40] = r_own[...]
    r[6:22, 40:48] = r_yhi[...]
    set_weights(q, w, diag, 1, 27, boxed)
    first_guess(e, c, q, w, r, 1, 27)
    sweep(e, c, e2, c2, q, w, r, 2, 26, boxed)
    sweep(e2, c2, e, c, q, w, r, 3, 25, boxed)

    def left(x):
        return (r[x] + flow(e, c, q, x, boxed) - diag[x] * e[x])[8:40]

    def body(i, carry):
        pairs[i] = left(6 + 2 * i) + left(7 + 2 * i)
        return carry

    lax.fori_loop(0, 8, body, 0, unroll=UNROLL // 2)
    r1 = 0.5 * halve(pairs[...]).reshape(8, 16, 128)
    r1_ref[...] = r1
    low_ref[...] = r1[:, :8]
    high_ref[...] = r1[:, 8:]


def down_one_kernel(
    own, xlo, xhi,
    q, w, r, e, out_ref,
    c, e2, c2, diag, pairs,
):
    z = iota((32, 128), 1)
    boxed = functools.partial(box, z=z, depth=128)
    for i, side in enumerate((xlo, own, xhi)):
        r[8 * i : 8 * i + 8] = side[0:8]
        q[8 * i : 8 * i + 8] = side[8:16]
    set_weights(q, w, diag, 1, 23, boxed)
    first_guess(e, c, q, w, r, 1, 23)
    sweep(e, c, e2, c2, q, w, r, 2, 22, boxed)
    sweep(e2, c2, e, c, q, w, r, 3, 21, boxed)

    def left(x):
        return (r[x] + flow(e, c, q, x, boxed) - diag[x] * e[x])[8:24]

    def body(i, carry):
        pairs[i] = left(8 + 2 * i) + left(9 + 2 * i)
        return carry

    lax.fori_loop(0, 4, body, 0, unroll=UNROLL // 2)
    r2 = 0.5 * pack_two(pairs[...])
    out_ref[...] = jnp.broadcast_to(r2[None], (DEVICES, 16, 128))


def ghosts(ref, count, group):
    lane = iota(ref.shape[1:], 1)
    ref[0] = jnp.where(lane >= group, pltpu.roll(ref[count], group, axis=1), 0.0)
    ref[count + 1] = jnp.where(lane < 128 - group, pltpu.roll(ref[1], 128 - group, axis=1), 0.0)


def assemble_two(gathered, ref):
    lane = iota((8, 128), 1)
    for bx in range(4):
        for by in range(NY):
            for j in range(2):
                a = gathered[bx * NY + by, j * 8 : j * 8 + 8]
                b = gathered[(bx + 4) * NY + by, j * 8 : j * 8 + 8]
                rows = slice(by * 8, by * 8 + 8)
                ref[1 + bx * 4 + j, rows] = jnp.where(lane < 64, a, pltpu.roll(b, 64, axis=1))
                ref[1 + bx * 4 + 2 + j, rows] = jnp.where(lane < 64, pltpu.roll(a, 64, axis=1), b)


def lane_maps():
    src, dst = iota((128, 128), 0), iota((128, 128), 1)
    return [as_bf16(src // 64 * 64 + at + src % 64 // 2 == dst) for at in (0, 32)]


def coarse_plane(low, high, maps):
    return dot_split(pair_rows(64, 128), split_dot(low, maps[0]) + split_dot(high, maps[1]))


def boxes():
    z2, rows2 = iota((128, 128), 1) % 64, iota((128, 128), 0)
    z3, rows3 = iota((64, 128), 1) % 32, iota((64, 128), 0)
    return (
        functools.partial(box, z=z2, depth=64, rows=rows2),
        functools.partial(box, z=z3, depth=32, rows=rows3),
    )


def setup_kernel(q2_all, q2, w2, d2, q3, w3):
    boxed2, boxed3 = boxes()
    assemble_two(q2_all, q2)
    ghosts(q2, 16, 64)
    set_weights(q2, w2, d2, 1, 17, boxed2)
    maps = lane_maps()
    for x in range(4):
        q3[1 + x] = 0.125 * coarse_plane(
            q2[1 + 2 * x] + q2[2 + 2 * x], q2[9 + 2 * x] + q2[10 + 2 * x], maps
        )
    ghosts(q3, 4, 32)
    set_weights(q3, w3, None, 1, 5, boxed3)


def up_kernel(
    place_ref, r2_all, q2, w2, d2, q3, w3, q1, w1, r1, e1, q0, w0, r0, e0,
    column_ref, depth_ref, factor_ref,
    grid_ref, back_ref,
    r2, a2, ca2, b2, cb2,
    r3, a3, ca3, b3, cb3,
    last2, s1, c1, t1, ct1, s0, c0, t0, ct0, hi_ref, lo_ref, slots_ref, last0,
):
    bx, by = place_ref[0], place_ref[1]
    boxed2, boxed3 = boxes()
    assemble_two(r2_all, r2)
    first_guess(a2, ca2, q2, w2, r2, 1, 17)

    def sweep2(e, c, e_to, c_to):
        ghosts(e, 16, 64)
        ghosts(c, 16, 64)
        sweep(e, c, e_to, c_to, q2, w2, r2, 1, 17, boxed2)

    sweep2(a2, ca2, b2, cb2)
    sweep2(b2, cb2, a2, ca2)
    ghosts(a2, 16, 64)
    ghosts(ca2, 16, 64)
    maps = lane_maps()

    def left(x):
        return r2[x] + flow(a2, ca2, q2, x, boxed2) - d2[x] * a2[x]

    for x in range(4):
        r3[1 + x] = 0.5 * coarse_plane(
            left(1 + 2 * x) + left(2 + 2 * x), left(9 + 2 * x) + left(10 + 2 * x), maps
        )
    first_guess(a3, ca3, q3, w3, r3, 1, 5)
    now, later = (a3, ca3), (b3, cb3)
    for _ in range(7):
        ghosts(now[0], 4, 32)
        ghosts(now[1], 4, 32)
        sweep(*now, *later, q3, w3, r3, 1, 5, boxed3)
        now, later = later, now
    e3 = now[0]
    src, dst = iota((128, 128), 1), iota((128, 128), 0)
    lane_back = [as_bf16(src // 64 * 64 + at + src % 64 // 2 == dst) for at in (0, 32)]
    rows_double = as_bf16(iota((128, 64), 0) // 2 == iota((128, 64), 1))
    for x in range(8):
        more = dot_split(rows_double, split_dot(e3[1 + x % 4], lane_back[x // 4]))
        for j in (1 + 2 * x, 2 + 2 * x):
            new = a2[j] + more
            a2[j] = new
            ca2[j] = q2[j] * new
    sweep2(a2, ca2, b2, cb2)
    sweep2(b2, cb2, a2, ca2)
    ghosts(a2, 16, 64)
    ghosts(ca2, 16, 64)
    last2[:, 0:8] = jnp.zeros((16, 8, 128), F32)
    last2[:, 136:144] = jnp.zeros((16, 8, 128), F32)

    def final2(x, carry):
        last2[x - 1, 8:136] = 0.4 * a2[x] + w2[x] * (r2[x] + flow(a2, ca2, q2, x, boxed2))
        return carry

    lax.fori_loop(1, 17, final2, 0, unroll=UNROLL)
    z1 = iota((32, 128), 1)
    boxed1 = functools.partial(box, z=z1, depth=128)
    widen_lanes = as_bf16(iota((128, 128), 1) // 2 == iota((128, 128), 0))
    widen_rows = as_bf16((iota((32, 24), 0) + 8) // 2 == iota((32, 24), 1))
    for j in range(10):
        x = bx * 4 - 3 + j
        inside = jnp.logical_and(x >= 0, x < 32)
        at = jnp.clip(x, 0, 31)
        window = last2[lax.rem(at, 16), pl.ds(pl.multiple_of(by * 8, 8), 24), :]
        window = jnp.where(at >= 16, pltpu.roll(window, 64, axis=1), window)
        window = jnp.where(inside, window, 0.0)
        more = dot_split(widen_rows, split_dot(window, widen_lanes))
        for p in (2 * j + 2, 2 * j + 3):
            if 3 <= p < 21:
                new = e1[p] + more
                s1[p] = new
                c1[p] = q1[p] * new
    sweep(s1, c1, t1, ct1, q1, w1, r1, 4, 20, boxed1)
    sweep(t1, ct1, s1, c1, q1, w1, r1, 5, 19, boxed1)
    sweep(s1, c1, t1, None, q1, w1, r1, 6, 18, boxed1)
    boxed0 = box_parity
    wide_rows = as_bf16((iota((48, 32), 0) + 8) // 2 == iota((48, 32), 1))

    def widen(j, carry):
        more = dot_split(wide_rows, t1[6 + j])
        more = jnp.concatenate([more, more], axis=1)
        for p in (2 * j + 2, 2 * j + 3):
            new = e0[p] + more
            s0[p] = new
            c0[p] = q0[p] * new
        return carry

    lax.fori_loop(0, 12, widen, 0, unroll=UNROLL)
    sweep(s0, c0, t0, ct0, q0, w0, r0, 4, 24, boxed0)
    sweep(t0, ct0, s0, c0, q0, w0, r0, 5, 23, boxed0)

    def final0(x, carry):
        new = 0.4 * s0[x] + w0[x] * (r0[x] + flow(s0, c0, q0, x, boxed0))
        last0[x - 6] = new[8:40]
        return carry

    lax.fori_loop(6, 22, final0, 0, unroll=UNROLL)
    last = last0[...].reshape(512, 256)
    grid_ref[...] = split_dot(last, parity(1)).reshape(16, 32, 256)
    grid = jnp.transpose(last)
    up, down = scale_of(grid)
    hi, lo = two_parts(grid * up)
    hi_ref[...] = hi
    lo_ref[...] = lo.astype(F8)
    columns = iota16((512, CHUNK), 0)
    depths = iota((256, CHUNK), 0)

    def step(i, carry):
        at = pl.ds(pl.multiple_of(i * CHUNK, CHUNK), CHUNK)
        total = jnp.zeros((1, CHUNK), F32)
        for k in range(4):
            hot = hot16(columns, row16(column_ref[k : k + 1, at]))
            found = dot(hi_ref[...], hot) + dot(lo_ref[...], hot.astype(F8))
            here = depths == depth_lane(depth_ref[k : k + 1, at])
            picked = jnp.sum(jnp.where(here, found, 0.0), axis=0, keepdims=True)
            total = total + factor_ref[k : k + 1, at] * picked
        total = total * down
        for j in range(CHUNK // GROUP):
            slots_ref[pl.ds(i * (CHUNK // GROUP) + j, 1), :] = total[:, j * GROUP : (j + 1) * GROUP]
        return carry

    lax.fori_loop(0, SLOTS // CHUNK, step, 0)
    from_groups(slots_ref, back_ref)


def struct(*shape, dtype=F32):
    return jax.ShapeDtypeStruct(shape, dtype)


def call(kernel, outs, *args, smem=0, scratch=()):
    vmem = pl.BlockSpec(memory_space=pltpu.VMEM)
    return pl.pallas_call(
        kernel,
        out_shape=outs,
        in_specs=[pl.BlockSpec(memory_space=pltpu.SMEM)] * smem + [vmem] * (len(args) - smem),
        out_specs=tuple(vmem for _ in outs),
        scratch_shapes=[pltpu.VMEM(s, d) for s, d in scratch],
        compiler_params=pltpu.CompilerParams(vmem_limit_bytes=VMEM_BYTES),
    )(*args)


def swap(to_lower, to_upper, axis, count):
    up = [(i, i + 1) for i in range(count - 1)]
    down = [(j, i) for i, j in up]
    return lax.ppermute(to_upper, axis, up), lax.ppermute(to_lower, axis, down)


def shards(values, dest, active, column, depth, factor, base, state):
    dest = dest.reshape(64, 128)
    outgoing, rank = call(
        rank_kernel,
        (struct(DEVICES, LANES), struct(64, 128, dtype=jnp.int32)),
        active, dest, values.reshape(64, 128),
        smem=1, scratch=(((DEVICES, 256), F32), ((DEVICES, LANES), F32)),
    )
    outgoing, base, state = lax.optimization_barrier((outgoing, base, state))
    incoming = lax.all_to_all(outgoing, ("bx", "by"), split_axis=0, concat_axis=0, tiled=True)
    q, q1, q_low, q_high, q2 = call(
        kappa_kernel,
        (struct(16, 32, 256), struct(4, 16, 256), struct(20, 8, 256), struct(20, 8, 256), struct(16, 128)),
        base, state,
    )
    q2_all = lax.all_gather(q2[None], ("bx", "by"), axis=0, tiled=True)
    q_ylo, q_yhi = swap(q_low, q_high, "by", NY)
    rhs, r_low, r_high = call(
        deposit_kernel,
        (struct(16, 32, 256), struct(16, 8, 256), struct(16, 8, 256)),
        incoming, column, depth, factor,
        scratch=(((512, 256), F32), ((32, GROUP), F32)),
    )
    r_ylo, r_yhi = swap(r_low, r_high, "by", NY)

    def faces(r_planes, q_planes):
        return jnp.concatenate(
            [
                jnp.concatenate([lo[planes], own[planes], hi[planes]], axis=1)
                for lo, own, hi, planes in ((r_ylo, rhs, r_yhi, r_planes), (q_ylo, q, q_yhi, q_planes))
            ]
        )

    xlo, xhi = swap(faces(slice(0, 5), slice(0, 6)), faces(slice(11, 16), slice(10, 16)), "bx", NX)

    ext0, ext1 = (28, 48, 256), (24, 32, 128)
    q0e, w0e, r0e, e0e, r1, low1, high1 = call(
        down_kernel,
        (struct(*ext0),) * 4 + (struct(8, 16, 128), struct(8, 8, 128), struct(8, 8, 128)),
        q, q_ylo, q_yhi, rhs, r_ylo, r_yhi, xlo, xhi,
        scratch=((ext0, F32),) * 4 + (((8, 32, 256), F32),),
    )
    r1_ylo, r1_yhi = swap(low1, high1, "by", NY)
    q1_cat = jnp.concatenate([q_ylo[16:], q1, q_yhi[16:]], axis=1)
    q1_cat = jnp.concatenate([q1_cat[:, :, :128], q1_cat[:, :, 128:]])
    cat1 = jnp.concatenate([jnp.concatenate([r1_ylo, r1, r1_yhi], axis=1), q1_cat])
    xlo1, xhi1 = swap(cat1, cat1, "bx", NX)

    q1e, w1e, r1e, e1e, r2_out = call(
        down_one_kernel,
        (struct(*ext1),) * 4 + (struct(DEVICES, 16, 128),),
        cat1, xlo1, xhi1,
        scratch=((ext1, F32),) * 4 + (((4, 16, 128), F32),),
    )
    q2_all, r2_out = lax.optimization_barrier((q2_all, r2_out))
    r2_all = lax.all_to_all(r2_out, ("bx", "by"), split_axis=0, concat_axis=0, tiled=True)

    place = jnp.stack([lax.axis_index("bx"), lax.axis_index("by")]).astype(jnp.int32)
    whole2, whole3 = (18, 128, 128), (6, 64, 128)
    setup = call(setup_kernel, (struct(*whole2),) * 3 + (struct(*whole3),) * 2, q2_all)
    grid, back = call(
        up_kernel,
        (struct(16, 32, 256), struct(DEVICES, LANES)),
        place, r2_all, *setup, q1e, w1e, r1e, e1e, q0e, w0e, r0e, e0e, column, depth, factor,
        smem=1,
        scratch=((whole2, F32),) * 5
        + ((whole3, F32),) * 5
        + (((16, 144, 128), F32),)
        + ((ext1, F32),) * 4
        + ((ext0, F32),) * 4
        + (((256, 512), BF16), ((256, 512), F8), ((32, GROUP), F32), ((16, 32, 256), F32)),
    )
    returned = lax.all_to_all(back, ("bx", "by"), split_axis=0, concat_axis=0, tiled=True)
    (picked,) = call(pick_kernel, (struct(64, 128),), active, dest, rank, returned, smem=1)
    return grid, picked.reshape(ROWS)


def solution(mesh):
    placed = (
        P(("bx", "by")),
        P(("bx", "by"), None),
        P(("bx", "by")),
        P(None, ("bx", "by")),
        P(None, ("bx", "by")),
        P(None, ("bx", "by")),
        P("bx", "by", None),
        P("bx", "by", None),
    )
    return jax.shard_map(
        shards,
        mesh=mesh,
        in_specs=placed,
        out_specs=(P("bx", "by", None), P(("bx", "by"))),
        check_vma=False,
    )
```

```python
import functools

import jax
import jax.numpy as jnp
from jax import lax
from jax.experimental import pallas as pl
from jax.experimental.pallas import tpu as pltpu
from jax.sharding import Mesh
from jax.sharding import PartitionSpec as P

NX, NY = 8, 16
DEVICES = NX * NY
CHIPS = DEVICES // 2
BX = ("x", "core")
ALL = ("x", "core", "by")
CAP = 96
LANES = 128
ROWS = 8192
SLOTS = DEVICES * CAP
F32 = jnp.float32
BF16 = jnp.bfloat16
F8 = jnp.float8_e4m3fn
I16 = jnp.int16
UNROLL = 4
RANK_UNROLL = 16
VMEM_BYTES = 56 * 1024 * 1024


def iota(shape, dim):
    return lax.broadcasted_iota(jnp.int32, shape, dim)


def pieces(x, count):
    parts = []
    for _ in range(count):
        part = x.astype(BF16)
        parts.append(part)
        x = x - part.astype(F32)
    return parts


def dot(a, b):
    return jnp.dot(a, b, preferred_element_type=F32)


def dot_nt(a, b):
    return lax.dot_general(a, b, (((1,), (1,)), ((), ())), preferred_element_type=F32)


def split_dot(x, m, count=2):
    return sum(dot(p, m) for p in pieces(x, count))


def dot_split(m, x, count=2):
    return sum(dot(m, p) for p in pieces(x, count))


def as_bf16(mask):
    return jnp.where(mask, 1.0, 0.0).astype(BF16)


def row16(x):
    return jnp.broadcast_to(x, (16, x.shape[1])).astype(I16)[0:1]


def iota16(shape, dim):
    return iota(shape, dim).astype(I16)


def hot16(rows, row):
    return jnp.where(rows == row, jnp.ones((), BF16), jnp.zeros((), BF16))


def pair_rows(coarse, fine):
    return as_bf16(iota((coarse, fine), 1) // 2 == iota((coarse, fine), 0))


def pair_lanes(fine, coarse, at=0):
    return as_bf16(iota((fine, coarse), 0) // 2 + at == iota((fine, coarse), 1))


def rank_kernel(active_ref, dest_ref, value_ref, out_ref, rank_ref, run_ref, acc_ref):
    active = active_ref[0]
    wide = 256
    upper = as_bf16(iota((wide, wide), 0) < iota((wide, wide), 1))
    ones = jnp.ones((wide, wide), BF16)
    bricks = iota16((DEVICES, wide), 0)
    ranks = iota16((LANES, wide), 0)
    zero = jnp.zeros((), BF16)
    run_ref[...] = jnp.zeros_like(run_ref)
    acc_ref[...] = jnp.zeros_like(acc_ref)

    def step(i, carry):
        def row(ref):
            return jnp.concatenate([ref[pl.ds(2 * i, 1), :], ref[pl.ds(2 * i + 1, 1), :]], axis=1)

        live = i * wide + iota((1, wide), 1) < active
        dest = row16(jnp.where(live, row(dest_ref), -1))
        hot = hot16(bricks, dest)
        run = run_ref[...]
        rank = jnp.sum(hot.astype(F32) * (dot(hot, upper) + run), axis=0, keepdims=True)
        rank = rank.astype(jnp.int32)
        run_ref[...] = run + dot(hot, ones)
        rank_ref[pl.ds(2 * i, 1), :] = rank[:, :128]
        rank_ref[pl.ds(2 * i + 1, 1), :] = rank[:, 128:]
        at = ranks == row16(rank)
        total = acc_ref[...]
        for part in pieces(jnp.broadcast_to(row(value_ref), (16, wide)), 2):
            total = total + dot_nt(hot, jnp.where(at, part[0:1], zero))
        acc_ref[...] = total
        return carry

    lax.fori_loop(0, ROWS // wide, step, 0, unroll=RANK_UNROLL)
    out_ref[...] = acc_ref[...]


def pick_kernel(active_ref, dest_ref, rank_ref, back_ref, out_ref):
    active = active_ref[0]
    wide = 256
    bricks = iota16((DEVICES, wide), 0)
    ranks = iota((LANES, wide), 0)
    table = jnp.transpose(back_ref[...])
    hi, lo = pieces(table, 2)

    def step(i, carry):
        def row(ref):
            return jnp.concatenate([ref[pl.ds(2 * i, 1), :], ref[pl.ds(2 * i + 1, 1), :]], axis=1)

        live = i * wide + iota((1, wide), 1) < active
        hot = hot16(bricks, row16(jnp.where(live, row(dest_ref), -1)))
        columns = dot(hi, hot) + dot(lo, hot)
        picked = jnp.sum(jnp.where(ranks == row(rank_ref), columns, 0.0), axis=0, keepdims=True)
        out_ref[pl.ds(2 * i, 1), :] = picked[:, :128]
        out_ref[pl.ds(2 * i + 1, 1), :] = picked[:, 128:]
        return carry

    lax.fori_loop(0, ROWS // wide, step, 0, unroll=RANK_UNROLL)


CHUNK = 3072
GROUP = 4 * CAP


def to_groups(ref, out):
    a = [ref[pl.ds(i, 32, stride=4), :] for i in range(4)]
    lane = iota((32, 128), 1)

    def moved(x, by):
        return pltpu.roll(x, by, axis=1)

    out[:, 0:128] = jnp.where(lane < 96, a[0], moved(a[1], 96))
    out[:, 128:256] = jnp.where(lane < 64, moved(a[1], 96), moved(a[2], 64))
    out[:, 256:384] = jnp.where(lane < 32, moved(a[2], 64), moved(a[3], 32))


def from_groups(ref, out):
    t = [ref[:, 128 * i : 128 * i + 128] for i in range(3)]
    lane = iota((32, 128), 1)

    def moved(x, by):
        return pltpu.roll(x, by, axis=1)

    out[pl.ds(0, 32, stride=4), :] = t[0]
    out[pl.ds(1, 32, stride=4), :] = jnp.where(lane < 32, moved(t[0], 32), moved(t[1], 32))
    out[pl.ds(2, 32, stride=4), :] = jnp.where(lane < 64, moved(t[1], 64), moved(t[2], 64))
    out[pl.ds(3, 32, stride=4), :] = moved(t[2], 96)
TOP = 32768.0


def scale_of(x):
    largest = jnp.maximum(jnp.max(jnp.abs(x), axis=(0, 1), keepdims=True), 1e-30)
    return TOP / largest, largest * (1.0 / TOP)


def two_parts(x):
    hi = x.astype(BF16)
    return hi, x - hi.astype(F32)


def depth_lane(depth):
    return (depth & 1) * 128 + (depth >> 1)


def deposit_kernel(slots_ref, column_ref, depth_ref, factor_ref, rhs_ref, low_ref, high_ref, acc_ref, value_ref):
    to_groups(slots_ref, value_ref)
    up, down = scale_of(value_ref[...])
    acc_ref[...] = jnp.zeros_like(acc_ref)
    columns = iota16((512, CHUNK), 0)
    depths = iota16((256, CHUNK), 0)
    zero = jnp.zeros((), BF16)

    def step(i, carry):
        at = pl.ds(pl.multiple_of(i * CHUNK, CHUNK), CHUNK)
        groups = [value_ref[pl.ds(i * (CHUNK // GROUP) + j, 1), :] for j in range(CHUNK // GROUP)]
        value = jnp.concatenate(groups, axis=1) * up
        total = acc_ref[...]
        for k in range(4):
            amount = jnp.broadcast_to(factor_ref[k : k + 1, at] * value, (16, CHUNK))
            hi, lo = two_parts(amount)
            lo = lo.astype(BF16)
            hot = hot16(columns, row16(column_ref[k : k + 1, at]))
            here = depths == row16(depth_lane(depth_ref[k : k + 1, at]))
            total = total + dot_nt(hot, jnp.where(here, hi[0:1], zero))
            total = total + dot_nt(hot.astype(F8), jnp.where(here, lo[0:1], zero).astype(F8))
        acc_ref[...] = total
        return carry

    lax.fori_loop(0, SLOTS // CHUNK, step, 0)
    rhs = (acc_ref[...] * down).reshape(16, 32, 256)
    rhs_ref[...] = rhs
    low_ref[...] = rhs[:, :8]
    high_ref[...] = rhs[:, 24:]


def box(v, z, depth, rows=None):
    n, m = v.shape
    v = (
        v
        + jnp.where(z == 0, 0.0, pltpu.roll(v, 1, axis=1))
        + jnp.where(z == depth - 1, 0.0, pltpu.roll(v, m - 1, axis=1))
    )
    up, down = pltpu.roll(v, 1, axis=0), pltpu.roll(v, n - 1, axis=0)
    if rows is not None:
        up = jnp.where(rows == 0, 0.0, up)
        down = jnp.where(rows == n - 1, 0.0, down)
    return v + up + down


def box_parity(v, group=128, rows=None):
    n = v.shape[0]
    even, odd = v[:, :128], v[:, 128:]
    lane = iota((n, 128), 1) & (group - 1)
    both = even + odd
    before = jnp.where(lane == 0, 0.0, pltpu.roll(odd, 1, axis=1))
    after = jnp.where(lane == group - 1, 0.0, pltpu.roll(even, 127, axis=1))
    v = jnp.concatenate([both + before, both + after], axis=1)
    up, down = pltpu.roll(v, 1, axis=0), pltpu.roll(v, n - 1, axis=0)
    if rows is not None:
        up = jnp.where(rows == 0, 0.0, up)
        down = jnp.where(rows == n - 1, 0.0, down)
    return v + up + down


def parity(dim):
    z, lane = iota((256, 256), dim), iota((256, 256), 1 - dim)
    return as_bf16(z % 2 * 128 + z // 2 == lane)


def near(ref, x):
    return ref[x - 1] + ref[x] + ref[x + 1]


def flow(e, c, q, x, boxed):
    return q[x] * boxed(near(e, x)) + boxed(near(c, x)) - 2.0 * c[x]


def unroll_of(ref):
    return 2 if ref.shape[1] == 128 else UNROLL


def set_weights(q, w, diag, lo, hi, boxed):
    def body(x, carry):
        here = q[x]
        d = 27.6 * here + boxed(near(q, x))
        w[x] = jnp.where(here > 0.0, 0.6 / d, 0.0)
        if diag is not None:
            diag[x] = d
        return carry

    lax.fori_loop(lo, hi, body, 0, unroll=unroll_of(q))


def first_guess(e, c, q, w, r, lo, hi):
    def body(x, carry):
        first = w[x] * r[x]
        e[x] = first
        c[x] = q[x] * first
        return carry

    lax.fori_loop(lo, hi, body, 0, unroll=unroll_of(q))


def sweep(e, c, e2, c2, q, w, r, lo, hi, boxed):
    def body(x, carry):
        new = 0.4 * e[x] + w[x] * (r[x] + flow(e, c, q, x, boxed))
        e2[x] = new
        if c2 is not None:
            c2[x] = q[x] * new
        return carry

    lax.fori_loop(lo, hi, body, 0, unroll=unroll_of(q))


def pack_two(pairs):
    both = dot_split(pair_rows(32, 64), pairs.reshape(64, 128))
    flat = jnp.concatenate([both[8 * x : 8 * x + 8] for x in range(4)], axis=1)
    src, dst = iota((512, 256), 0), iota((512, 256), 1)
    z = src % 128 // 2
    lane = z % 2 * 128 + src // 128 * 32 + z // 2
    packed = split_dot(flat, as_bf16(lane == dst))
    return jnp.concatenate([packed[:, :128], packed[:, 128:]], axis=0)


def halve(pairs):
    flat = pairs.reshape(256, 256)
    return dot_split(pair_rows(128, 256), flat[:, :128] + flat[:, 128:])


def kappa_kernel(base_ref, state_ref, q_ref, q1_ref, low_ref, high_ref, q2_ref):
    q = base_ref[...] * jnp.exp(0.4 * state_ref[...]) * (1.0 / 52.0)
    q = split_dot(q.reshape(512, 256), parity(0)).reshape(16, 32, 256)
    q_ref[...] = q
    q1 = 0.125 * halve(jnp.sum(q.reshape(8, 2, 32, 256), axis=1)).reshape(8, 16, 128)
    packed = jnp.concatenate([q1[:4], q1[4:]], axis=2)
    q1_ref[...] = packed
    low_ref[0:16] = q[:, :8]
    high_ref[0:16] = q[:, 24:]
    low_ref[16:20] = packed[:, :8]
    high_ref[16:20] = packed[:, 8:]
    q2_ref[...] = 0.125 * pack_two(jnp.sum(q1.reshape(4, 2, 16, 128), axis=1))


def down_kernel(
    q_own, q_ylo, q_yhi, r_own, r_ylo, r_yhi, xlo, xhi,
    q_out, w_out, r_out, e_out, r1_ref, low_ref, high_ref,
    q, w, r, e, c, e2, c2, diag, pairs, sems,
):
    boxed = box_parity
    q[0:6] = xlo[5:11]
    q[22:28] = xhi[5:11]
    q[6:22, 0:8] = q_ylo[0:16]
    q[6:22, 8:40] = q_own[...]
    q[6:22, 40:48] = q_yhi[0:16]
    r[1:6] = xlo[0:5]
    r[22:27] = xhi[0:5]
    r[6:22, 0:8] = r_ylo[...]
    r[6:22, 8:40] = r_own[...]
    r[6:22, 40:48] = r_yhi[...]
    pairs_out = ((q, q_out), (r, r_out), (w, w_out), (e, e_out))
    copies = [pltpu.make_async_copy(a, b, sems.at[i]) for i, (a, b) in enumerate(pairs_out)]
    copies[0].start()
    copies[1].start()
    set_weights(q, w, diag, 1, 27, boxed)
    copies[2].start()
    first_guess(e, c, q, w, r, 1, 27)
    sweep(e, c, e2, c2, q, w, r, 2, 26, boxed)
    sweep(e2, c2, e, c, q, w, r, 3, 25, boxed)
    copies[3].start()

    def left(x):
        return (r[x] + flow(e, c, q, x, boxed) - diag[x] * e[x])[8:40]

    def body(i, carry):
        pairs[i] = left(6 + 2 * i) + left(7 + 2 * i)
        return carry

    lax.fori_loop(0, 8, body, 0, unroll=UNROLL // 2)
    r1 = 0.5 * halve(pairs[...]).reshape(8, 16, 128)
    r1_ref[...] = r1
    low_ref[...] = r1[:, :8]
    high_ref[...] = r1[:, 8:]
    for copy in copies:
        copy.wait()


def down_one_kernel(
    own, xlo, xhi,
    q, w, r, e, out_ref,
    c, e2, c2, diag, pairs,
):
    z = iota((32, 128), 1)
    boxed = functools.partial(box, z=z, depth=128)
    for i, side in enumerate((xlo, own, xhi)):
        r[8 * i : 8 * i + 8] = side[0:8]
        q[8 * i : 8 * i + 8] = side[8:16]
    set_weights(q, w, diag, 1, 23, boxed)
    first_guess(e, c, q, w, r, 1, 23)
    sweep(e, c, e2, c2, q, w, r, 2, 22, boxed)
    sweep(e2, c2, e, c, q, w, r, 3, 21, boxed)

    def left(x):
        return (r[x] + flow(e, c, q, x, boxed) - diag[x] * e[x])[8:24]

    def body(i, carry):
        pairs[i] = left(8 + 2 * i) + left(9 + 2 * i)
        return carry

    lax.fori_loop(0, 4, body, 0, unroll=UNROLL // 2)
    r2 = 0.5 * pack_two(pairs[...])
    out_ref[...] = jnp.broadcast_to(r2[None], (CHIPS, 16, 128))


def ghosts(ref, count, group):
    lane = iota((ref.shape[1], 128), 1)
    for at in range(0, ref.shape[2], 128):
        half = slice(at, at + 128)
        ref[0, :, half] = jnp.where(lane >= group, pltpu.roll(ref[count, :, half], group, axis=1), 0.0)
        ref[count + 1, :, half] = jnp.where(
            lane < 128 - group, pltpu.roll(ref[1, :, half], 128 - group, axis=1), 0.0
        )


def assemble_two(block, ref):
    lane = iota((16, 128), 1)
    low_half, low_quarter = lane < 64, (lane & 63) < 32

    def moved(x, by):
        return pltpu.roll(x, by, axis=1)

    def body(by, carry):
        rows = pl.ds(pl.multiple_of(by * 8, 8), 8)
        for h in range(2):
            a = [block(h, g, by) for g in range(4)]
            b = [None] * 4
            for i in range(2):
                b[i] = jnp.where(low_half, a[i], moved(a[i + 2], 64))
                b[i + 2] = jnp.where(low_half, moved(a[i], 64), a[i + 2])
            for i in (0, 2):
                first = jnp.where(low_quarter, b[i], moved(b[i + 1], 32))
                second = jnp.where(low_quarter, moved(b[i], 96), b[i + 1])
                for j, plane in ((i, first), (i + 1, second)):
                    ref[1 + h * 4 + j, rows, 0:128] = plane[0:8]
                    ref[1 + h * 4 + j, rows, 128:256] = plane[8:16]
        return carry

    lax.fori_loop(0, NY, body, 0, unroll=4)


def coarse_planes(planes):
    wide = jnp.concatenate([p[:, :128] + p[:, 128:] for p in planes], axis=1)
    thin = dot_split(pair_rows(64, 128), wide)
    return [thin[:, 128 * i : 128 * i + 128] for i in range(4)]


def boxes():
    z3, rows3 = iota((64, 128), 1) % 32, iota((64, 128), 0)
    return (
        functools.partial(box_parity, group=32, rows=iota((128, 256), 0)),
        functools.partial(box, z=z3, depth=32, rows=rows3),
    )


def setup_kernel(q2_all, q2, w2, d2, q3, w3):
    boxed2, boxed3 = boxes()
    assemble_two(lambda core, g, by: q2_all[(2 * g + core) * NY + by], q2)
    ghosts(q2, 8, 32)
    set_weights(q2, w2, d2, 1, 9, boxed2)
    for x, plane in enumerate(coarse_planes([q2[1 + 2 * x] + q2[2 + 2 * x] for x in range(4)])):
        q3[1 + x] = 0.125 * plane
    ghosts(q3, 4, 32)
    set_weights(q3, w3, None, 1, 5, boxed3)


def up_kernel(
    place_ref, r2_mine, r2_other, q2, w2, d2, q3, w3, *refs
):
    hbm, (grid_ref, back_ref) = refs[:11], refs[11:13]
    (
        r2, a2, ca2, b2, cb2,
        r3, a3, ca3, b3, cb3,
        last2, s1, c1, t1, ct1, s0, c0, t0, ct0, hi_ref, lo_ref, slots_ref, last0,
    ) = refs[13:36]
    local, sems = refs[36:47], refs[47]
    copies = [pltpu.make_async_copy(hbm[i], local[i], sems.at[i]) for i in range(11)]
    for copy in copies:
        copy.start()
    q1, w1, r1, e1, q0, w0, r0, e0, column_ref, depth_ref, factor_ref = local
    bx, by = place_ref[0], place_ref[1]
    boxed2, boxed3 = boxes()
    core = lax.rem(bx, 2)

    def block(of, g, by):
        i = g * NY + by
        return jnp.where(core == of, r2_mine[i], r2_other[i])

    assemble_two(block, r2)
    first_guess(a2, ca2, q2, w2, r2, 1, 9)

    def sweep2(e, c, e_to, c_to):
        ghosts(e, 8, 32)
        ghosts(c, 8, 32)
        sweep(e, c, e_to, c_to, q2, w2, r2, 1, 9, boxed2)

    sweep2(a2, ca2, b2, cb2)
    sweep2(b2, cb2, a2, ca2)
    ghosts(a2, 8, 32)
    ghosts(ca2, 8, 32)

    def left(x):
        return r2[x] + flow(a2, ca2, q2, x, boxed2) - d2[x] * a2[x]

    for x, plane in enumerate(coarse_planes([left(1 + 2 * x) + left(2 + 2 * x) for x in range(4)])):
        r3[1 + x] = 0.5 * plane
    first_guess(a3, ca3, q3, w3, r3, 1, 5)
    now, later = (a3, ca3), (b3, cb3)
    for _ in range(7):
        ghosts(now[0], 4, 32)
        ghosts(now[1], 4, 32)
        sweep(*now, *later, q3, w3, r3, 1, 5, boxed3)
        now, later = later, now
    e3 = now[0]
    rows_double = as_bf16(iota((128, 64), 0) // 2 == iota((128, 64), 1))
    more = dot_split(rows_double, jnp.concatenate([e3[1 + x] for x in range(4)], axis=1))
    for j in range(1, 9):
        add = more[:, (j - 1) // 2 * 128 : (j - 1) // 2 * 128 + 128]
        new = a2[j] + jnp.concatenate([add, add], axis=1)
        a2[j] = new
        ca2[j] = q2[j] * new
    sweep2(a2, ca2, b2, cb2)
    sweep2(b2, cb2, a2, ca2)
    ghosts(a2, 8, 32)
    ghosts(ca2, 8, 32)
    last2[:, 0:8] = jnp.zeros((8, 8, 256), F32)
    last2[:, 136:144] = jnp.zeros((8, 8, 256), F32)

    def final2(x, carry):
        last2[x - 1, 8:136] = 0.4 * a2[x] + w2[x] * (r2[x] + flow(a2, ca2, q2, x, boxed2))
        return carry

    lax.fori_loop(1, 9, final2, 0, unroll=2)
    z1 = iota((32, 128), 1)
    boxed1 = functools.partial(box, z=z1, depth=128)
    src, dst = iota((256, 128), 0), iota((256, 128), 1)
    widen_lanes = as_bf16(jnp.logical_and(dst // 4 == src % 128, dst // 2 % 2 == src // 128))
    widen_rows = as_bf16((iota((32, 24), 0) + 8) // 2 == iota((32, 24), 1))
    windows = []
    for j in range(10):
        x = bx * 4 - 3 + j
        inside = jnp.logical_and(x >= 0, x < 32)
        at = jnp.clip(x, 0, 31)
        rows = pl.ds(pl.multiple_of(by * 8, 8), 24)
        shift = lax.rem(128 - at // 8 * 32, 128)
        halves = [
            pltpu.roll(last2[lax.rem(at, 8), rows, lanes : lanes + 128], shift, axis=1) for lanes in (0, 128)
        ]
        windows.append(jnp.where(inside, jnp.concatenate(halves, axis=1), 0.0))
    wide = split_dot(jnp.concatenate(windows, axis=0), widen_lanes)
    wide = jnp.concatenate([wide[24 * j : 24 * j + 24] for j in range(10)], axis=1)
    wide = dot_split(widen_rows, wide)
    for copy in copies[:4]:
        copy.wait()
    for p in range(3, 21):
        j = (p - 2) // 2
        new = e1[p] + wide[:, 128 * j : 128 * j + 128]
        s1[p] = new
        c1[p] = q1[p] * new
    sweep(s1, c1, t1, ct1, q1, w1, r1, 4, 20, boxed1)
    sweep(t1, ct1, s1, c1, q1, w1, r1, 5, 19, boxed1)
    sweep(s1, c1, t1, None, q1, w1, r1, 6, 18, boxed1)
    boxed0 = box_parity
    wide_rows = as_bf16((iota((48, 32), 0) + 8) // 2 == iota((48, 32), 1))

    wide = dot_split(wide_rows, jnp.concatenate([t1[6 + j] for j in range(12)], axis=1))
    for copy in copies[4:]:
        copy.wait()
    for p in range(3, 25):
        add = wide[:, (p - 2) // 2 * 128 : (p - 2) // 2 * 128 + 128]
        new = e0[p] + jnp.concatenate([add, add], axis=1)
        s0[p] = new
        c0[p] = q0[p] * new
    sweep(s0, c0, t0, ct0, q0, w0, r0, 4, 24, boxed0)
    sweep(t0, ct0, s0, c0, q0, w0, r0, 5, 23, boxed0)

    def final0(x, carry):
        new = 0.4 * s0[x] + w0[x] * (r0[x] + flow(s0, c0, q0, x, boxed0))
        last0[x - 6] = new[8:40]
        return carry

    lax.fori_loop(6, 22, final0, 0, unroll=UNROLL)
    last = last0[...].reshape(512, 256)
    grid_ref[...] = split_dot(last, parity(1)).reshape(16, 32, 256)
    grid = jnp.transpose(last)
    up, down = scale_of(grid)
    hi, lo = two_parts(grid * up)
    hi_ref[...] = hi
    lo_ref[...] = lo.astype(F8)
    columns = iota16((512, CHUNK), 0)
    depths = iota((256, CHUNK), 0)

    def step(i, carry):
        at = pl.ds(pl.multiple_of(i * CHUNK, CHUNK), CHUNK)
        total = jnp.zeros((1, CHUNK), F32)
        for k in range(4):
            hot = hot16(columns, row16(column_ref[k : k + 1, at]))
            found = dot(hi_ref[...], hot) + dot(lo_ref[...], hot.astype(F8))
            here = depths == depth_lane(depth_ref[k : k + 1, at])
            picked = jnp.sum(jnp.where(here, found, 0.0), axis=0, keepdims=True)
            total = total + factor_ref[k : k + 1, at] * picked
        total = total * down
        for j in range(CHUNK // GROUP):
            slots_ref[pl.ds(i * (CHUNK // GROUP) + j, 1), :] = total[:, j * GROUP : (j + 1) * GROUP]
        return carry

    lax.fori_loop(0, SLOTS // CHUNK, step, 0)
    from_groups(slots_ref, back_ref)


def struct(*shape, dtype=F32):
    return jax.ShapeDtypeStruct(shape, dtype)


def call(kernel, outs, *args, smem=0, left=0, left_out=0, scratch=()):
    vmem = pl.BlockSpec(memory_space=pltpu.VMEM)
    return pl.pallas_call(
        kernel,
        out_shape=outs,
        in_specs=[pl.BlockSpec(memory_space=pltpu.SMEM)] * smem
        + [vmem] * (len(args) - smem - left)
        + [pl.BlockSpec(memory_space=pl.ANY)] * left,
        out_specs=tuple(pl.BlockSpec(memory_space=pl.ANY) if i < left_out else vmem for i in range(len(outs))),
        scratch_shapes=[pltpu.VMEM(s, d) for s, d in scratch]
        + ([pltpu.VMEM(a.shape, a.dtype) for a in args[-left:]] + [pltpu.SemaphoreType.DMA((left,))] if left else [])
        + ([pltpu.SemaphoreType.DMA((left_out,))] if left_out else []),
        compiler_params=pltpu.CompilerParams(vmem_limit_bytes=VMEM_BYTES),
    )(*args)


def swap(to_lower, to_upper, axis, count):
    up = [(i, i + 1) for i in range(count - 1)]
    down = [(j, i) for i, j in up]
    return lax.ppermute(to_upper, axis, up), lax.ppermute(to_lower, axis, down)


def shards(values, dest, active, column, depth, factor, base, state):
    dest = dest.reshape(64, 128)
    outgoing, rank = call(
        rank_kernel,
        (struct(DEVICES, LANES), struct(64, 128, dtype=jnp.int32)),
        active, dest, values.reshape(64, 128),
        smem=1, scratch=(((DEVICES, 256), F32), ((DEVICES, LANES), F32)),
    )
    incoming = lax.all_to_all(outgoing, ALL, split_axis=0, concat_axis=0, tiled=True)
    q, q1, q_low, q_high, q2 = call(
        kappa_kernel,
        (struct(16, 32, 256), struct(4, 16, 256), struct(20, 8, 256), struct(20, 8, 256), struct(16, 128)),
        base, state,
    )
    q2_all = lax.all_gather(q2[None], ALL, axis=0, tiled=True)
    q_ylo, q_yhi = swap(q_low, q_high, "by", NY)
    rhs, r_low, r_high = call(
        deposit_kernel,
        (struct(16, 32, 256), struct(16, 8, 256), struct(16, 8, 256)),
        incoming, column, depth, factor,
        scratch=(((512, 256), F32), ((32, GROUP), F32)),
    )
    r_ylo, r_yhi = swap(r_low, r_high, "by", NY)

    def faces(r_planes, q_planes):
        return jnp.concatenate(
            [
                jnp.concatenate([lo[planes], own[planes], hi[planes]], axis=1)
                for lo, own, hi, planes in ((r_ylo, rhs, r_yhi, r_planes), (q_ylo, q, q_yhi, q_planes))
            ]
        )

    xlo, xhi = swap(faces(slice(0, 5), slice(0, 6)), faces(slice(11, 16), slice(10, 16)), BX, NX)

    ext0, ext1 = (28, 48, 256), (24, 32, 128)
    q0e, w0e, r0e, e0e, r1, low1, high1 = call(
        down_kernel,
        (struct(*ext0),) * 4 + (struct(8, 16, 128), struct(8, 8, 128), struct(8, 8, 128)),
        q, q_ylo, q_yhi, rhs, r_ylo, r_yhi, xlo, xhi,
        left_out=4,
        scratch=((ext0, F32),) * 8 + (((8, 32, 256), F32),),
    )
    r1_ylo, r1_yhi = swap(low1, high1, "by", NY)
    q1_cat = jnp.concatenate([q_ylo[16:], q1, q_yhi[16:]], axis=1)
    q1_cat = jnp.concatenate([q1_cat[:, :, :128], q1_cat[:, :, 128:]])
    cat1 = jnp.concatenate([jnp.concatenate([r1_ylo, r1, r1_yhi], axis=1), q1_cat])
    xlo1, xhi1 = swap(cat1, cat1, BX, NX)

    q1e, w1e, r1e, e1e, r2_out = call(
        down_one_kernel,
        (struct(*ext1),) * 4 + (struct(CHIPS, 16, 128),),
        cat1, xlo1, xhi1,
        scratch=((ext1, F32),) * 4 + (((4, 16, 128), F32),),
    )
    q2_all, r2_out = lax.optimization_barrier((q2_all, r2_out))
    r2_mine = lax.all_to_all(r2_out, ("x", "by"), split_axis=0, concat_axis=0, tiled=True)
    whole2, whole3 = (10, 128, 256), (6, 64, 128)
    setup = call(setup_kernel, (struct(*whole2),) * 3 + (struct(*whole3),) * 2, q2_all)
    r2_mine, setup = lax.optimization_barrier((r2_mine, setup))
    r2_other = lax.ppermute(r2_mine, "core", [(0, 1), (1, 0)])

    place = jnp.stack([lax.axis_index(BX), lax.axis_index("by")]).astype(jnp.int32)
    grid, back = call(
        up_kernel,
        (struct(16, 32, 256), struct(DEVICES, LANES)),
        place, r2_mine, r2_other, *setup, q1e, w1e, r1e, e1e, q0e, w0e, r0e, e0e, column, depth, factor,
        smem=1,
        left=11,
        scratch=((whole2, F32),) * 5
        + ((whole3, F32),) * 5
        + (((8, 144, 256), F32),)
        + ((ext1, F32),) * 4
        + ((ext0, F32),) * 4
        + (((256, 512), BF16), ((256, 512), F8), ((32, GROUP), F32), ((16, 32, 256), F32)),
    )
    returned = lax.all_to_all(back, ALL, split_axis=0, concat_axis=0, tiled=True)
    (picked,) = call(pick_kernel, (struct(64, 128),), active, dest, rank, returned, smem=1)
    return grid, picked.reshape(ROWS)


def solution(mesh):
    placed = (
        P(ALL),
        P(ALL, None),
        P(ALL),
        P(None, ALL),
        P(None, ALL),
        P(None, ALL),
        P(BX, "by", None),
        P(BX, "by", None),
    )
    mesh = Mesh(mesh.devices.reshape(NX // 2, 2, NY), ALL)
    return jax.shard_map(
        shards,
        mesh=mesh,
        in_specs=placed,
        out_specs=(P(BX, "by", None), P(ALL)),
        check_vma=False,
    )
```

```python
import functools

import jax
import jax.numpy as jnp
from jax import lax
from jax.experimental import pallas as pl
from jax.experimental.pallas import tpu as pltpu
from jax.sharding import Mesh
from jax.sharding import PartitionSpec as P

NX, NY = 8, 16
DEVICES = NX * NY
CHIPS = DEVICES // 2
BX = ("x", "core")
ALL = ("x", "core", "by")
CAP = 96
LANES = 128
ROWS = 8192
SLOTS = DEVICES * CAP
F32 = jnp.float32
BF16 = jnp.bfloat16
F8 = jnp.float8_e4m3fn
I16 = jnp.int16
UNROLL = 4
RANK_UNROLL = 16
VMEM_BYTES = 56 * 1024 * 1024


def iota(shape, dim):
    return lax.broadcasted_iota(jnp.int32, shape, dim)


def pieces(x, count):
    parts = []
    for _ in range(count):
        part = x.astype(BF16)
        parts.append(part)
        x = x - part.astype(F32)
    return parts


def dot(a, b):
    return jnp.dot(a, b, preferred_element_type=F32)


def dot_nt(a, b):
    return lax.dot_general(a, b, (((1,), (1,)), ((), ())), preferred_element_type=F32)


def split_dot(x, m, count=2):
    return sum(dot(p, m) for p in pieces(x, count))


def dot_split(m, x, count=2):
    return sum(dot(m, p) for p in pieces(x, count))


def as_bf16(mask):
    return jnp.where(mask, 1.0, 0.0).astype(BF16)


def row16(x):
    return jnp.broadcast_to(x, (16, x.shape[1])).astype(I16)[0:1]


def iota16(shape, dim):
    return iota(shape, dim).astype(I16)


def hot16(rows, row):
    return jnp.where(rows == row, jnp.ones((), BF16), jnp.zeros((), BF16))


def pair_rows(coarse, fine):
    return as_bf16(iota((coarse, fine), 1) // 2 == iota((coarse, fine), 0))


def pair_lanes(fine, coarse, at=0):
    return as_bf16(iota((fine, coarse), 0) // 2 + at == iota((fine, coarse), 1))


def rank_kernel(active_ref, dest_ref, value_ref, out_ref, rank_ref, run_ref, acc_ref):
    active = active_ref[0]
    wide = 256
    upper = as_bf16(iota((wide, wide), 0) < iota((wide, wide), 1))
    ones = jnp.ones((wide, wide), BF16)
    bricks = iota16((DEVICES, wide), 0)
    ranks = iota16((LANES, wide), 0)
    zero = jnp.zeros((), BF16)
    run_ref[...] = jnp.zeros_like(run_ref)
    acc_ref[...] = jnp.zeros_like(acc_ref)

    def step(i, carry):
        def row(ref):
            return jnp.concatenate([ref[pl.ds(2 * i, 1), :], ref[pl.ds(2 * i + 1, 1), :]], axis=1)

        live = i * wide + iota((1, wide), 1) < active
        dest = row16(jnp.where(live, row(dest_ref), -1))
        hot = hot16(bricks, dest)
        run = run_ref[...]
        rank = jnp.sum(hot.astype(F32) * (dot(hot, upper) + run), axis=0, keepdims=True)
        rank = rank.astype(jnp.int32)
        run_ref[...] = run + dot(hot, ones)
        rank_ref[pl.ds(2 * i, 1), :] = rank[:, :128]
        rank_ref[pl.ds(2 * i + 1, 1), :] = rank[:, 128:]
        at = ranks == row16(rank)
        total = acc_ref[...]
        for part in pieces(jnp.broadcast_to(row(value_ref), (16, wide)), 2):
            total = total + dot_nt(hot, jnp.where(at, part[0:1], zero))
        acc_ref[...] = total
        return carry

    lax.fori_loop(0, ROWS // wide, step, 0, unroll=RANK_UNROLL)
    out_ref[...] = acc_ref[...]


def pick_kernel(active_ref, dest_ref, rank_ref, back_ref, out_ref):
    active = active_ref[0]
    wide = 256
    bricks = iota16((DEVICES, wide), 0)
    ranks = iota((LANES, wide), 0)
    table = jnp.transpose(back_ref[...])
    hi, lo = pieces(table, 2)

    def step(i, carry):
        def row(ref):
            return jnp.concatenate([ref[pl.ds(2 * i, 1), :], ref[pl.ds(2 * i + 1, 1), :]], axis=1)

        live = i * wide + iota((1, wide), 1) < active
        hot = hot16(bricks, row16(jnp.where(live, row(dest_ref), -1)))
        columns = dot(hi, hot) + dot(lo, hot)
        picked = jnp.sum(jnp.where(ranks == row(rank_ref), columns, 0.0), axis=0, keepdims=True)
        out_ref[pl.ds(2 * i, 1), :] = picked[:, :128]
        out_ref[pl.ds(2 * i + 1, 1), :] = picked[:, 128:]
        return carry

    lax.fori_loop(0, ROWS // wide, step, 0, unroll=RANK_UNROLL)


CHUNK = 3072
GROUP = 4 * CAP


def to_groups(ref, out):
    a = [ref[pl.ds(i, 32, stride=4), :] for i in range(4)]
    lane = iota((32, 128), 1)

    def moved(x, by):
        return pltpu.roll(x, by, axis=1)

    out[:, 0:128] = jnp.where(lane < 96, a[0], moved(a[1], 96))
    out[:, 128:256] = jnp.where(lane < 64, moved(a[1], 96), moved(a[2], 64))
    out[:, 256:384] = jnp.where(lane < 32, moved(a[2], 64), moved(a[3], 32))


def from_groups(ref, out):
    t = [ref[:, 128 * i : 128 * i + 128] for i in range(3)]
    lane = iota((32, 128), 1)

    def moved(x, by):
        return pltpu.roll(x, by, axis=1)

    out[pl.ds(0, 32, stride=4), :] = t[0]
    out[pl.ds(1, 32, stride=4), :] = jnp.where(lane < 32, moved(t[0], 32), moved(t[1], 32))
    out[pl.ds(2, 32, stride=4), :] = jnp.where(lane < 64, moved(t[1], 64), moved(t[2], 64))
    out[pl.ds(3, 32, stride=4), :] = moved(t[2], 96)
TOP = 32768.0


def scale_of(x):
    largest = jnp.maximum(jnp.max(jnp.abs(x), axis=(0, 1), keepdims=True), 1e-30)
    return TOP / largest, largest * (1.0 / TOP)


def two_parts(x):
    hi = x.astype(BF16)
    return hi, x - hi.astype(F32)


def depth_lane(depth):
    return (depth & 1) * 128 + (depth >> 1)


def deposit_kernel(slots_ref, column_ref, depth_ref, factor_ref, rhs_ref, low_ref, high_ref, acc_ref, value_ref):
    to_groups(slots_ref, value_ref)
    up, down = scale_of(value_ref[...])
    acc_ref[...] = jnp.zeros_like(acc_ref)
    columns = iota16((512, CHUNK), 0)
    depths = iota16((256, CHUNK), 0)
    zero = jnp.zeros((), BF16)

    def step(i, carry):
        at = pl.ds(pl.multiple_of(i * CHUNK, CHUNK), CHUNK)
        groups = [value_ref[pl.ds(i * (CHUNK // GROUP) + j, 1), :] for j in range(CHUNK // GROUP)]
        value = jnp.concatenate(groups, axis=1) * up
        total = acc_ref[...]
        for k in range(4):
            amount = jnp.broadcast_to(factor_ref[k : k + 1, at] * value, (16, CHUNK))
            hi, lo = two_parts(amount)
            lo = lo.astype(BF16)
            hot = hot16(columns, row16(column_ref[k : k + 1, at]))
            here = depths == row16(depth_lane(depth_ref[k : k + 1, at]))
            total = total + dot_nt(hot, jnp.where(here, hi[0:1], zero))
            total = total + dot_nt(hot.astype(F8), jnp.where(here, lo[0:1], zero).astype(F8))
        acc_ref[...] = total
        return carry

    lax.fori_loop(0, SLOTS // CHUNK, step, 0)
    rhs = (acc_ref[...] * down).reshape(16, 32, 256)
    rhs_ref[...] = rhs
    low_ref[...] = rhs[:, :8]
    high_ref[...] = rhs[:, 24:]


def box(v, z, depth, rows=None):
    n, m = v.shape
    v = (
        v
        + jnp.where(z == 0, 0.0, pltpu.roll(v, 1, axis=1))
        + jnp.where(z == depth - 1, 0.0, pltpu.roll(v, m - 1, axis=1))
    )
    up, down = pltpu.roll(v, 1, axis=0), pltpu.roll(v, n - 1, axis=0)
    if rows is not None:
        up = jnp.where(rows == 0, 0.0, up)
        down = jnp.where(rows == n - 1, 0.0, down)
    return v + up + down


def box_parity(v, group=128, rows=None):
    n = v.shape[0]
    even, odd = v[:, :128], v[:, 128:]
    lane = iota((n, 128), 1) & (group - 1)
    both = even + odd
    before = jnp.where(lane == 0, 0.0, pltpu.roll(odd, 1, axis=1))
    after = jnp.where(lane == group - 1, 0.0, pltpu.roll(even, 127, axis=1))
    v = jnp.concatenate([both + before, both + after], axis=1)
    up, down = pltpu.roll(v, 1, axis=0), pltpu.roll(v, n - 1, axis=0)
    if rows is not None:
        up = jnp.where(rows == 0, 0.0, up)
        down = jnp.where(rows == n - 1, 0.0, down)
    return v + up + down


def parity(dim):
    z, lane = iota((256, 256), dim), iota((256, 256), 1 - dim)
    return as_bf16(z % 2 * 128 + z // 2 == lane)


def near(ref, x):
    return ref[x - 1] + ref[x] + ref[x + 1]


def flow(e, c, q, x, boxed):
    return q[x] * boxed(near(e, x)) + boxed(near(c, x)) - 2.0 * c[x]


def unroll_of(ref):
    return 2 if ref.shape[1] == 128 else UNROLL


def set_weights(q, w, diag, lo, hi, boxed):
    def body(x, carry):
        here = q[x]
        d = 27.6 * here + boxed(near(q, x))
        w[x] = jnp.where(here > 0.0, 0.6 / d, 0.0)
        if diag is not None:
            diag[x] = d
        return carry

    lax.fori_loop(lo, hi, body, 0, unroll=unroll_of(q))


def first_guess(e, c, q, w, r, lo, hi):
    def body(x, carry):
        first = w[x] * r[x]
        e[x] = first
        c[x] = q[x] * first
        return carry

    lax.fori_loop(lo, hi, body, 0, unroll=unroll_of(q))


def sweep(e, c, e2, c2, q, w, r, lo, hi, boxed):
    def body(x, carry):
        new = 0.4 * e[x] + w[x] * (r[x] + flow(e, c, q, x, boxed))
        e2[x] = new
        if c2 is not None:
            c2[x] = q[x] * new
        return carry

    lax.fori_loop(lo, hi, body, 0, unroll=unroll_of(q))


def pack_two(pairs):
    both = dot_split(pair_rows(32, 64), pairs.reshape(64, 128))
    flat = jnp.concatenate([both[8 * x : 8 * x + 8] for x in range(4)], axis=1)
    src, dst = iota((512, 256), 0), iota((512, 256), 1)
    z = src % 128 // 2
    lane = z % 2 * 128 + src // 128 * 32 + z // 2
    packed = split_dot(flat, as_bf16(lane == dst))
    return jnp.concatenate([packed[:, :128], packed[:, 128:]], axis=0)


def halve(pairs):
    flat = pairs.reshape(256, 256)
    return dot_split(pair_rows(128, 256), flat[:, :128] + flat[:, 128:])


def kappa_kernel(base_ref, state_ref, q_ref, q1_ref, low_ref, high_ref, q2_ref):
    q = base_ref[...] * jnp.exp(0.4 * state_ref[...]) * (1.0 / 52.0)
    q = split_dot(q.reshape(512, 256), parity(0)).reshape(16, 32, 256)
    q_ref[...] = q
    q1 = 0.125 * halve(jnp.sum(q.reshape(8, 2, 32, 256), axis=1)).reshape(8, 16, 128)
    packed = jnp.concatenate([q1[:4], q1[4:]], axis=2)
    q1_ref[...] = packed
    low_ref[0:16] = q[:, :8]
    high_ref[0:16] = q[:, 24:]
    low_ref[16:20] = packed[:, :8]
    high_ref[16:20] = packed[:, 8:]
    q2_ref[...] = 0.125 * pack_two(jnp.sum(q1.reshape(4, 2, 16, 128), axis=1))


def down_kernel(
    q_own, q_ylo, q_yhi, q_xlo, q_xhi, r_own, r_ylo, r_yhi, r_xlo, r_xhi,
    q_out, w_out, r_out, e_out, r1_ref, low_ref, high_ref,
    q, w, r, e, c, e2, c2, diag, pairs, sems,
):
    boxed = box_parity
    q[0:6] = q_xlo[0:288].reshape(6, 48, 256)
    q[22:28] = q_xhi[0:288].reshape(6, 48, 256)
    q[6:22, 0:8] = q_ylo[0:16]
    q[6:22, 8:40] = q_own[...]
    q[6:22, 40:48] = q_yhi[0:16]
    r[1:6] = r_xlo[...]
    r[22:27] = r_xhi[...]
    r[6:22, 0:8] = r_ylo[...]
    r[6:22, 8:40] = r_own[...]
    r[6:22, 40:48] = r_yhi[...]
    pairs_out = ((q, q_out), (r, r_out), (w, w_out), (e, e_out))
    copies = [pltpu.make_async_copy(a, b, sems.at[i]) for i, (a, b) in enumerate(pairs_out)]
    copies[0].start()
    copies[1].start()
    set_weights(q, w, diag, 1, 27, boxed)
    copies[2].start()
    first_guess(e, c, q, w, r, 1, 27)
    sweep(e, c, e2, c2, q, w, r, 2, 26, boxed)
    sweep(e2, c2, e, c, q, w, r, 3, 25, boxed)
    copies[3].start()

    def left(x):
        return (r[x] + flow(e, c, q, x, boxed) - diag[x] * e[x])[8:40]

    def body(i, carry):
        pairs[i] = left(6 + 2 * i) + left(7 + 2 * i)
        return carry

    lax.fori_loop(0, 8, body, 0, unroll=UNROLL // 2)
    r1 = 0.5 * halve(pairs[...]).reshape(8, 16, 128)
    r1_ref[...] = r1
    low_ref[...] = r1[:, :8]
    high_ref[...] = r1[:, 8:]
    for copy in copies:
        copy.wait()


def down_one_kernel(
    own, xlo, xhi, q_own, q_xlo, q_xhi,
    q, w, r, e, out_ref,
    c, e2, c2, diag, pairs,
):
    z = iota((32, 128), 1)
    boxed = functools.partial(box, z=z, depth=128)
    for i, side in enumerate((xlo, own, xhi)):
        r[8 * i : 8 * i + 8] = side[...]
    for i, side in enumerate((q_xlo[288:416].reshape(4, 32, 256), q_own[...], q_xhi[288:416].reshape(4, 32, 256))):
        q[8 * i : 8 * i + 4] = side[:, :, :128]
        q[8 * i + 4 : 8 * i + 8] = side[:, :, 128:]
    set_weights(q, w, diag, 1, 23, boxed)
    first_guess(e, c, q, w, r, 1, 23)
    sweep(e, c, e2, c2, q, w, r, 2, 22, boxed)
    sweep(e2, c2, e, c, q, w, r, 3, 21, boxed)

    def left(x):
        return (r[x] + flow(e, c, q, x, boxed) - diag[x] * e[x])[8:24]

    def body(i, carry):
        pairs[i] = left(8 + 2 * i) + left(9 + 2 * i)
        return carry

    lax.fori_loop(0, 4, body, 0, unroll=UNROLL // 2)
    r2 = 0.5 * pack_two(pairs[...])
    out_ref[...] = jnp.broadcast_to(r2[None], (CHIPS, 16, 128))


def ghosts(ref, count, group):
    lane = iota((ref.shape[1], 128), 1)
    for at in range(0, ref.shape[2], 128):
        half = slice(at, at + 128)
        ref[0, :, half] = jnp.where(lane >= group, pltpu.roll(ref[count, :, half], group, axis=1), 0.0)
        ref[count + 1, :, half] = jnp.where(
            lane < 128 - group, pltpu.roll(ref[1, :, half], 128 - group, axis=1), 0.0
        )


def assemble_two(block, ref):
    lane = iota((16, 128), 1)
    low_half, low_quarter = lane < 64, (lane & 63) < 32

    def moved(x, by):
        return pltpu.roll(x, by, axis=1)

    def body(by, carry):
        rows = pl.ds(pl.multiple_of(by * 8, 8), 8)
        for h in range(2):
            a = [block(h, g, by) for g in range(4)]
            b = [None] * 4
            for i in range(2):
                b[i] = jnp.where(low_half, a[i], moved(a[i + 2], 64))
                b[i + 2] = jnp.where(low_half, moved(a[i], 64), a[i + 2])
            for i in (0, 2):
                first = jnp.where(low_quarter, b[i], moved(b[i + 1], 32))
                second = jnp.where(low_quarter, moved(b[i], 96), b[i + 1])
                for j, plane in ((i, first), (i + 1, second)):
                    ref[1 + h * 4 + j, rows, 0:128] = plane[0:8]
                    ref[1 + h * 4 + j, rows, 128:256] = plane[8:16]
        return carry

    lax.fori_loop(0, NY, body, 0, unroll=4)


def coarse_planes(planes):
    wide = jnp.concatenate([p[:, :128] + p[:, 128:] for p in planes], axis=1)
    thin = dot_split(pair_rows(64, 128), wide)
    return [thin[:, 128 * i : 128 * i + 128] for i in range(4)]


def boxes():
    z3, rows3 = iota((64, 128), 1) % 32, iota((64, 128), 0)
    return (
        functools.partial(box_parity, group=32, rows=iota((128, 256), 0)),
        functools.partial(box, z=z3, depth=32, rows=rows3),
    )


def setup_kernel(q2_all, q2, w2, d2, q3, w3):
    boxed2, boxed3 = boxes()
    assemble_two(lambda core, g, by: q2_all[(2 * g + core) * NY + by], q2)
    ghosts(q2, 8, 32)
    set_weights(q2, w2, d2, 1, 9, boxed2)
    for x, plane in enumerate(coarse_planes([q2[1 + 2 * x] + q2[2 + 2 * x] for x in range(4)])):
        q3[1 + x] = 0.125 * plane
    ghosts(q3, 4, 32)
    set_weights(q3, w3, None, 1, 5, boxed3)


def up_kernel(
    place_ref, r2_mine, r2_other, q2, w2, d2, q3, w3, *refs
):
    hbm, (grid_ref, back_ref) = refs[:11], refs[11:13]
    (
        r2, a2, ca2, b2, cb2,
        r3, a3, ca3, b3, cb3,
        last2, s1, c1, t1, ct1, s0, c0, t0, ct0, hi_ref, lo_ref, slots_ref, last0,
    ) = refs[13:36]
    local, sems = refs[36:47], refs[47]
    copies = [pltpu.make_async_copy(hbm[i], local[i], sems.at[i]) for i in range(11)]
    for copy in copies:
        copy.start()
    q1, w1, r1, e1, q0, w0, r0, e0, column_ref, depth_ref, factor_ref = local
    bx, by = place_ref[0], place_ref[1]
    boxed2, boxed3 = boxes()
    core = lax.rem(bx, 2)

    def block(of, g, by):
        i = g * NY + by
        return jnp.where(core == of, r2_mine[i], r2_other[i])

    assemble_two(block, r2)
    first_guess(a2, ca2, q2, w2, r2, 1, 9)

    def sweep2(e, c, e_to, c_to):
        ghosts(e, 8, 32)
        ghosts(c, 8, 32)
        sweep(e, c, e_to, c_to, q2, w2, r2, 1, 9, boxed2)

    sweep2(a2, ca2, b2, cb2)
    sweep2(b2, cb2, a2, ca2)
    ghosts(a2, 8, 32)
    ghosts(ca2, 8, 32)

    def left(x):
        return r2[x] + flow(a2, ca2, q2, x, boxed2) - d2[x] * a2[x]

    for x, plane in enumerate(coarse_planes([left(1 + 2 * x) + left(2 + 2 * x) for x in range(4)])):
        r3[1 + x] = 0.5 * plane
    first_guess(a3, ca3, q3, w3, r3, 1, 5)
    now, later = (a3, ca3), (b3, cb3)
    for _ in range(7):
        ghosts(now[0], 4, 32)
        ghosts(now[1], 4, 32)
        sweep(*now, *later, q3, w3, r3, 1, 5, boxed3)
        now, later = later, now
    e3 = now[0]
    rows_double = as_bf16(iota((128, 64), 0) // 2 == iota((128, 64), 1))
    more = dot_split(rows_double, jnp.concatenate([e3[1 + x] for x in range(4)], axis=1))
    for j in range(1, 9):
        add = more[:, (j - 1) // 2 * 128 : (j - 1) // 2 * 128 + 128]
        new = a2[j] + jnp.concatenate([add, add], axis=1)
        a2[j] = new
        ca2[j] = q2[j] * new
    sweep2(a2, ca2, b2, cb2)
    sweep2(b2, cb2, a2, ca2)
    ghosts(a2, 8, 32)
    ghosts(ca2, 8, 32)
    last2[:, 0:8] = jnp.zeros((8, 8, 256), F32)
    last2[:, 136:144] = jnp.zeros((8, 8, 256), F32)

    def final2(x, carry):
        last2[x - 1, 8:136] = 0.4 * a2[x] + w2[x] * (r2[x] + flow(a2, ca2, q2, x, boxed2))
        return carry

    lax.fori_loop(1, 9, final2, 0, unroll=2)
    z1 = iota((32, 128), 1)
    boxed1 = functools.partial(box, z=z1, depth=128)
    src, dst = iota((256, 128), 0), iota((256, 128), 1)
    widen_lanes = as_bf16(jnp.logical_and(dst // 4 == src % 128, dst // 2 % 2 == src // 128))
    widen_rows = as_bf16((iota((32, 24), 0) + 8) // 2 == iota((32, 24), 1))
    windows = []
    for j in range(10):
        x = bx * 4 - 3 + j
        inside = jnp.logical_and(x >= 0, x < 32)
        at = jnp.clip(x, 0, 31)
        rows = pl.ds(pl.multiple_of(by * 8, 8), 24)
        shift = lax.rem(128 - at // 8 * 32, 128)
        halves = [
            pltpu.roll(last2[lax.rem(at, 8), rows, lanes : lanes + 128], shift, axis=1) for lanes in (0, 128)
        ]
        windows.append(jnp.where(inside, jnp.concatenate(halves, axis=1), 0.0))
    wide = split_dot(jnp.concatenate(windows, axis=0), widen_lanes)
    wide = jnp.concatenate([wide[24 * j : 24 * j + 24] for j in range(10)], axis=1)
    wide = dot_split(widen_rows, wide)
    for copy in copies[:4]:
        copy.wait()
    for p in range(3, 21):
        j = (p - 2) // 2
        new = e1[p] + wide[:, 128 * j : 128 * j + 128]
        s1[p] = new
        c1[p] = q1[p] * new
    sweep(s1, c1, t1, ct1, q1, w1, r1, 4, 20, boxed1)
    sweep(t1, ct1, s1, c1, q1, w1, r1, 5, 19, boxed1)
    sweep(s1, c1, t1, None, q1, w1, r1, 6, 18, boxed1)
    boxed0 = box_parity
    wide_rows = as_bf16((iota((48, 32), 0) + 8) // 2 == iota((48, 32), 1))

    wide = dot_split(wide_rows, jnp.concatenate([t1[6 + j] for j in range(12)], axis=1))
    for copy in copies[4:]:
        copy.wait()
    for p in range(3, 25):
        add = wide[:, (p - 2) // 2 * 128 : (p - 2) // 2 * 128 + 128]
        new = e0[p] + jnp.concatenate([add, add], axis=1)
        s0[p] = new
        c0[p] = q0[p] * new
    sweep(s0, c0, t0, ct0, q0, w0, r0, 4, 24, boxed0)
    sweep(t0, ct0, s0, c0, q0, w0, r0, 5, 23, boxed0)

    def final0(x, carry):
        new = 0.4 * s0[x] + w0[x] * (r0[x] + flow(s0, c0, q0, x, boxed0))
        last0[x - 6] = new[8:40]
        return carry

    lax.fori_loop(6, 22, final0, 0, unroll=UNROLL)
    last = last0[...].reshape(512, 256)
    grid_ref[...] = split_dot(last, parity(1)).reshape(16, 32, 256)
    grid = jnp.transpose(last)
    up, down = scale_of(grid)
    hi, lo = two_parts(grid * up)
    hi_ref[...] = hi
    lo_ref[...] = lo.astype(F8)
    columns = iota16((512, CHUNK), 0)
    depths = iota((256, CHUNK), 0)

    def step(i, carry):
        at = pl.ds(pl.multiple_of(i * CHUNK, CHUNK), CHUNK)
        total = jnp.zeros((1, CHUNK), F32)
        for k in range(4):
            hot = hot16(columns, row16(column_ref[k : k + 1, at]))
            found = dot(hi_ref[...], hot) + dot(lo_ref[...], hot.astype(F8))
            here = depths == depth_lane(depth_ref[k : k + 1, at])
            picked = jnp.sum(jnp.where(here, found, 0.0), axis=0, keepdims=True)
            total = total + factor_ref[k : k + 1, at] * picked
        total = total * down
        for j in range(CHUNK // GROUP):
            slots_ref[pl.ds(i * (CHUNK // GROUP) + j, 1), :] = total[:, j * GROUP : (j + 1) * GROUP]
        return carry

    lax.fori_loop(0, SLOTS // CHUNK, step, 0)
    from_groups(slots_ref, back_ref)


def struct(*shape, dtype=F32):
    return jax.ShapeDtypeStruct(shape, dtype)


def call(kernel, outs, *args, smem=0, left=0, left_out=0, scratch=()):
    vmem = pl.BlockSpec(memory_space=pltpu.VMEM)
    return pl.pallas_call(
        kernel,
        out_shape=outs,
        in_specs=[pl.BlockSpec(memory_space=pltpu.SMEM)] * smem
        + [vmem] * (len(args) - smem - left)
        + [pl.BlockSpec(memory_space=pl.ANY)] * left,
        out_specs=tuple(pl.BlockSpec(memory_space=pl.ANY) if i < left_out else vmem for i in range(len(outs))),
        scratch_shapes=[pltpu.VMEM(s, d) for s, d in scratch]
        + ([pltpu.VMEM(a.shape, a.dtype) for a in args[-left:]] + [pltpu.SemaphoreType.DMA((left,))] if left else [])
        + ([pltpu.SemaphoreType.DMA((left_out,))] if left_out else []),
        compiler_params=pltpu.CompilerParams(vmem_limit_bytes=VMEM_BYTES),
    )(*args)


def swap(to_lower, to_upper, axis, count):
    up = [(i, i + 1) for i in range(count - 1)]
    down = [(j, i) for i, j in up]
    return lax.ppermute(to_upper, axis, up), lax.ppermute(to_lower, axis, down)


def shards(values, dest, active, column, depth, factor, base, state):
    dest = dest.reshape(64, 128)
    outgoing, rank = call(
        rank_kernel,
        (struct(DEVICES, LANES), struct(64, 128, dtype=jnp.int32)),
        active, dest, values.reshape(64, 128),
        smem=1, scratch=(((DEVICES, 256), F32), ((DEVICES, LANES), F32)),
    )
    incoming = lax.all_to_all(outgoing, ALL, split_axis=0, concat_axis=0, tiled=True)
    q, q1, q_low, q_high, q2 = call(
        kappa_kernel,
        (struct(16, 32, 256), struct(4, 16, 256), struct(20, 8, 256), struct(20, 8, 256), struct(16, 128)),
        base, state,
    )
    q2_all = lax.all_gather(q2[None], ALL, axis=0, tiled=True)
    q_ylo, q_yhi = swap(q_low, q_high, "by", NY)

    def faces(lo, own, hi, planes):
        return jnp.concatenate([lo[planes], own[planes], hi[planes]], axis=1)

    q1_cat = faces(q_ylo[16:], q1, q_yhi[16:], slice(0, 4))

    def q_faces(planes):
        return jnp.concatenate([faces(q_ylo, q, q_yhi, planes).reshape(288, 256), q1_cat.reshape(128, 256)])

    q_xlo, q_xhi = swap(q_faces(slice(0, 6)), q_faces(slice(10, 16)), BX, NX)

    rhs, r_low, r_high = call(
        deposit_kernel,
        (struct(16, 32, 256), struct(16, 8, 256), struct(16, 8, 256)),
        incoming, column, depth, factor,
        scratch=(((512, 256), F32), ((32, GROUP), F32)),
    )
    r_ylo, r_yhi = swap(r_low, r_high, "by", NY)
    r_xlo, r_xhi = swap(
        faces(r_ylo, rhs, r_yhi, slice(0, 5)), faces(r_ylo, rhs, r_yhi, slice(11, 16)), BX, NX
    )

    ext0, ext1 = (28, 48, 256), (24, 32, 128)
    q0e, w0e, r0e, e0e, r1, low1, high1 = call(
        down_kernel,
        (struct(*ext0),) * 4 + (struct(8, 16, 128), struct(8, 8, 128), struct(8, 8, 128)),
        q, q_ylo, q_yhi, q_xlo, q_xhi, rhs, r_ylo, r_yhi, r_xlo, r_xhi,
        left_out=4,
        scratch=((ext0, F32),) * 8 + (((8, 32, 256), F32),),
    )
    r1_ylo, r1_yhi = swap(low1, high1, "by", NY)
    cat1 = jnp.concatenate([r1_ylo, r1, r1_yhi], axis=1)
    xlo1, xhi1 = swap(cat1, cat1, BX, NX)

    q1e, w1e, r1e, e1e, r2_out = call(
        down_one_kernel,
        (struct(*ext1),) * 4 + (struct(CHIPS, 16, 128),),
        cat1, xlo1, xhi1, q1_cat, q_xlo, q_xhi,
        scratch=((ext1, F32),) * 4 + (((4, 16, 128), F32),),
    )
    q2_all, r2_out = lax.optimization_barrier((q2_all, r2_out))
    r2_mine = lax.all_to_all(r2_out, ("x", "by"), split_axis=0, concat_axis=0, tiled=True)
    whole2, whole3 = (10, 128, 256), (6, 64, 128)
    setup = call(setup_kernel, (struct(*whole2),) * 3 + (struct(*whole3),) * 2, q2_all)
    r2_mine, setup = lax.optimization_barrier((r2_mine, setup))
    r2_other = lax.ppermute(r2_mine, "core", [(0, 1), (1, 0)])

    place = jnp.stack([lax.axis_index(BX), lax.axis_index("by")]).astype(jnp.int32)
    grid, back = call(
        up_kernel,
        (struct(16, 32, 256), struct(DEVICES, LANES)),
        place, r2_mine, r2_other, *setup, q1e, w1e, r1e, e1e, q0e, w0e, r0e, e0e, column, depth, factor,
        smem=1,
        left=11,
        scratch=((whole2, F32),) * 5
        + ((whole3, F32),) * 5
        + (((8, 144, 256), F32),)
        + ((ext1, F32),) * 4
        + ((ext0, F32),) * 4
        + (((256, 512), BF16), ((256, 512), F8), ((32, GROUP), F32), ((16, 32, 256), F32)),
    )
    returned = lax.all_to_all(back, ALL, split_axis=0, concat_axis=0, tiled=True)
    (picked,) = call(pick_kernel, (struct(64, 128),), active, dest, rank, returned, smem=1)
    return grid, picked.reshape(ROWS)


def solution(mesh):
    placed = (
        P(ALL),
        P(ALL, None),
        P(ALL),
        P(None, ALL),
        P(None, ALL),
        P(None, ALL),
        P(BX, "by", None),
        P(BX, "by", None),
    )
    mesh = Mesh(mesh.devices.reshape(NX // 2, 2, NY), ALL)
    return jax.shard_map(
        shards,
        mesh=mesh,
        in_specs=placed,
        out_specs=(P(BX, "by", None), P(ALL)),
        check_vma=False,
    )
```

```python
import functools

import jax
import jax.numpy as jnp
from jax import lax
from jax.experimental import pallas as pl
from jax.experimental.pallas import tpu as pltpu
from jax.sharding import Mesh
from jax.sharding import PartitionSpec as P

NX, NY = 8, 16
DEVICES = NX * NY
CHIPS = DEVICES // 2
BX = ("x", "core")
ALL = ("x", "core", "by")
CAP = 96
LANES = 128
ROWS = 8192
SLOTS = DEVICES * CAP
F32 = jnp.float32
BF16 = jnp.bfloat16
F8 = jnp.float8_e4m3fn
I16 = jnp.int16
UNROLL = 4
RANK_UNROLL = 16
VMEM_BYTES = 56 * 1024 * 1024


def iota(shape, dim):
    return lax.broadcasted_iota(jnp.int32, shape, dim)


def pieces(x, count):
    parts = []
    for _ in range(count):
        part = x.astype(BF16)
        parts.append(part)
        x = x - part.astype(F32)
    return parts


def dot(a, b):
    return jnp.dot(a, b, preferred_element_type=F32)


def dot_nt(a, b):
    return lax.dot_general(a, b, (((1,), (1,)), ((), ())), preferred_element_type=F32)


def split_dot(x, m, count=2):
    return sum(dot(p, m) for p in pieces(x, count))


def dot_split(m, x, count=2):
    return sum(dot(m, p) for p in pieces(x, count))


def as_bf16(mask):
    return jnp.where(mask, 1.0, 0.0).astype(BF16)


def row16(x):
    return jnp.broadcast_to(x, (16, x.shape[1])).astype(I16)[0:1]


def iota16(shape, dim):
    return iota(shape, dim).astype(I16)


def hot16(rows, row):
    return jnp.where(rows == row, jnp.ones((), BF16), jnp.zeros((), BF16))


def pair_rows(coarse, fine):
    return as_bf16(iota((coarse, fine), 1) // 2 == iota((coarse, fine), 0))


def pair_lanes(fine, coarse, at=0):
    return as_bf16(iota((fine, coarse), 0) // 2 + at == iota((fine, coarse), 1))


def rank_kernel(active_ref, dest_ref, value_ref, out_ref, rank_ref, run_ref, acc_ref):
    active = active_ref[0]
    wide = 256
    upper = as_bf16(iota((wide, wide), 0) < iota((wide, wide), 1))
    ones = jnp.ones((wide, wide), BF16)
    bricks = iota16((DEVICES, wide), 0)
    ranks = iota16((LANES, wide), 0)
    zero = jnp.zeros((), BF16)
    run_ref[...] = jnp.zeros_like(run_ref)
    acc_ref[...] = jnp.zeros_like(acc_ref)

    def step(i, carry):
        def row(ref):
            return jnp.concatenate([ref[pl.ds(2 * i, 1), :], ref[pl.ds(2 * i + 1, 1), :]], axis=1)

        live = i * wide + iota((1, wide), 1) < active
        dest = row16(jnp.where(live, row(dest_ref), -1))
        hot = hot16(bricks, dest)
        run = run_ref[...]
        rank = jnp.sum(hot.astype(F32) * (dot(hot, upper) + run), axis=0, keepdims=True)
        rank = rank.astype(jnp.int32)
        run_ref[...] = run + dot(hot, ones)
        rank_ref[pl.ds(2 * i, 1), :] = rank[:, :128]
        rank_ref[pl.ds(2 * i + 1, 1), :] = rank[:, 128:]
        at = ranks == row16(rank)
        total = acc_ref[...]
        for part in pieces(jnp.broadcast_to(row(value_ref), (16, wide)), 2):
            total = total + dot_nt(hot, jnp.where(at, part[0:1], zero))
        acc_ref[...] = total
        return carry

    lax.fori_loop(0, ROWS // wide, step, 0, unroll=RANK_UNROLL)
    out_ref[...] = acc_ref[...]


def pick_kernel(active_ref, dest_ref, rank_ref, back_ref, out_ref):
    active = active_ref[0]
    wide = 256
    bricks = iota16((DEVICES, wide), 0)
    ranks = iota((LANES, wide), 0)
    table = jnp.transpose(back_ref[...])
    hi, lo = pieces(table, 2)

    def step(i, carry):
        def row(ref):
            return jnp.concatenate([ref[pl.ds(2 * i, 1), :], ref[pl.ds(2 * i + 1, 1), :]], axis=1)

        live = i * wide + iota((1, wide), 1) < active
        hot = hot16(bricks, row16(jnp.where(live, row(dest_ref), -1)))
        columns = dot(hi, hot) + dot(lo, hot)
        picked = jnp.sum(jnp.where(ranks == row(rank_ref), columns, 0.0), axis=0, keepdims=True)
        out_ref[pl.ds(2 * i, 1), :] = picked[:, :128]
        out_ref[pl.ds(2 * i + 1, 1), :] = picked[:, 128:]
        return carry

    lax.fori_loop(0, ROWS // wide, step, 0, unroll=RANK_UNROLL)


CHUNK = 3072
GROUP = 4 * CAP


def to_groups(ref, out):
    a = [ref[pl.ds(i, 32, stride=4), :] for i in range(4)]
    lane = iota((32, 128), 1)

    def moved(x, by):
        return pltpu.roll(x, by, axis=1)

    out[:, 0:128] = jnp.where(lane < 96, a[0], moved(a[1], 96))
    out[:, 128:256] = jnp.where(lane < 64, moved(a[1], 96), moved(a[2], 64))
    out[:, 256:384] = jnp.where(lane < 32, moved(a[2], 64), moved(a[3], 32))


def from_groups(ref, out):
    t = [ref[:, 128 * i : 128 * i + 128] for i in range(3)]
    lane = iota((32, 128), 1)

    def moved(x, by):
        return pltpu.roll(x, by, axis=1)

    out[pl.ds(0, 32, stride=4), :] = t[0]
    out[pl.ds(1, 32, stride=4), :] = jnp.where(lane < 32, moved(t[0], 32), moved(t[1], 32))
    out[pl.ds(2, 32, stride=4), :] = jnp.where(lane < 64, moved(t[1], 64), moved(t[2], 64))
    out[pl.ds(3, 32, stride=4), :] = moved(t[2], 96)
TOP = 32768.0


def scale_of(x):
    largest = jnp.maximum(jnp.max(jnp.abs(x), axis=(0, 1), keepdims=True), 1e-30)
    return TOP / largest, largest * (1.0 / TOP)


def two_parts(x):
    hi = x.astype(BF16)
    return hi, x - hi.astype(F32)


def depth_lane(depth):
    return (depth & 1) * 128 + (depth >> 1)


def deposit_kernel(slots_ref, column_ref, depth_ref, factor_ref, rhs_ref, low_ref, high_ref, acc_ref, value_ref):
    to_groups(slots_ref, value_ref)
    up, down = scale_of(value_ref[...])
    acc_ref[...] = jnp.zeros_like(acc_ref)
    columns = iota16((512, CHUNK), 0)
    depths = iota16((256, CHUNK), 0)
    zero = jnp.zeros((), BF16)

    def step(i, carry):
        at = pl.ds(pl.multiple_of(i * CHUNK, CHUNK), CHUNK)
        groups = [value_ref[pl.ds(i * (CHUNK // GROUP) + j, 1), :] for j in range(CHUNK // GROUP)]
        value = jnp.concatenate(groups, axis=1) * up
        total = acc_ref[...]
        for k in range(4):
            amount = jnp.broadcast_to(factor_ref[k : k + 1, at] * value, (16, CHUNK))
            hi, lo = two_parts(amount)
            lo = lo.astype(BF16)
            hot = hot16(columns, row16(column_ref[k : k + 1, at]))
            here = depths == row16(depth_lane(depth_ref[k : k + 1, at]))
            total = total + dot_nt(hot, jnp.where(here, hi[0:1], zero))
            total = total + dot_nt(hot.astype(F8), jnp.where(here, lo[0:1], zero).astype(F8))
        acc_ref[...] = total
        return carry

    lax.fori_loop(0, SLOTS // CHUNK, step, 0)
    rhs = (acc_ref[...] * down).reshape(16, 32, 256)
    rhs_ref[...] = rhs
    low_ref[...] = rhs[:, :8]
    high_ref[...] = rhs[:, 24:]


def box(v, z, depth, rows=None):
    n, m = v.shape
    v = (
        v
        + jnp.where(z == 0, 0.0, pltpu.roll(v, 1, axis=1))
        + jnp.where(z == depth - 1, 0.0, pltpu.roll(v, m - 1, axis=1))
    )
    up, down = pltpu.roll(v, 1, axis=0), pltpu.roll(v, n - 1, axis=0)
    if rows is not None:
        up = jnp.where(rows == 0, 0.0, up)
        down = jnp.where(rows == n - 1, 0.0, down)
    return v + up + down


def box_parity(v, group=128, rows=None):
    n = v.shape[0]
    even, odd = v[:, :128], v[:, 128:]
    lane = iota((n, 128), 1) & (group - 1)
    both = even + odd
    before = jnp.where(lane == 0, 0.0, pltpu.roll(odd, 1, axis=1))
    after = jnp.where(lane == group - 1, 0.0, pltpu.roll(even, 127, axis=1))
    v = jnp.concatenate([both + before, both + after], axis=1)
    up, down = pltpu.roll(v, 1, axis=0), pltpu.roll(v, n - 1, axis=0)
    if rows is not None:
        up = jnp.where(rows == 0, 0.0, up)
        down = jnp.where(rows == n - 1, 0.0, down)
    return v + up + down


def parity(dim):
    z, lane = iota((256, 256), dim), iota((256, 256), 1 - dim)
    return as_bf16(z % 2 * 128 + z // 2 == lane)


def near(ref, x):
    return ref[x - 1] + ref[x] + ref[x + 1]


def flow(e, c, q, x, boxed):
    return q[x] * boxed(near(e, x)) + boxed(near(c, x)) - 2.0 * c[x]


def unroll_of(ref):
    return 2 if ref.shape[1] == 128 else UNROLL


def set_weights(q, w, diag, lo, hi, boxed):
    def body(x, carry):
        here = q[x]
        d = 27.6 * here + boxed(near(q, x))
        w[x] = jnp.where(here > 0.0, 0.6 / d, 0.0)
        if diag is not None:
            diag[x] = d
        return carry

    lax.fori_loop(lo, hi, body, 0, unroll=unroll_of(q))


def first_guess(e, c, q, w, r, lo, hi):
    def body(x, carry):
        first = w[x] * r[x]
        e[x] = first
        c[x] = q[x] * first
        return carry

    lax.fori_loop(lo, hi, body, 0, unroll=unroll_of(q))


def sweep(e, c, e2, c2, q, w, r, lo, hi, boxed, unroll=None):
    def body(x, carry):
        new = 0.4 * e[x] + w[x] * (r[x] + flow(e, c, q, x, boxed))
        e2[x] = new
        if c2 is not None:
            c2[x] = q[x] * new
        return carry

    lax.fori_loop(lo, hi, body, 0, unroll=unroll or unroll_of(q))


def pack_two(pairs):
    both = dot_split(pair_rows(32, 64), pairs.reshape(64, 128))
    flat = jnp.concatenate([both[8 * x : 8 * x + 8] for x in range(4)], axis=1)
    src, dst = iota((512, 256), 0), iota((512, 256), 1)
    z = src % 128 // 2
    lane = z % 2 * 128 + src // 128 * 32 + z // 2
    packed = split_dot(flat, as_bf16(lane == dst))
    return jnp.concatenate([packed[:, :128], packed[:, 128:]], axis=0)


def halve(pairs):
    flat = pairs.reshape(256, 256)
    return dot_split(pair_rows(128, 256), flat[:, :128] + flat[:, 128:])


def kappa_kernel(base_ref, state_ref, q_ref, q1_ref, low_ref, high_ref, q2_ref):
    q = base_ref[...] * jnp.exp(0.4 * state_ref[...]) * (1.0 / 52.0)
    q = split_dot(q.reshape(512, 256), parity(0)).reshape(16, 32, 256)
    q_ref[...] = q
    q1 = 0.125 * halve(jnp.sum(q.reshape(8, 2, 32, 256), axis=1)).reshape(8, 16, 128)
    packed = jnp.concatenate([q1[:4], q1[4:]], axis=2)
    q1_ref[...] = packed
    low_ref[0:16] = q[:, :8]
    high_ref[0:16] = q[:, 24:]
    low_ref[16:20] = packed[:, :8]
    high_ref[16:20] = packed[:, 8:]
    q2_ref[...] = 0.125 * pack_two(jnp.sum(q1.reshape(4, 2, 16, 128), axis=1))


def down_kernel(
    q_own, q_ylo, q_yhi, q_xlo, q_xhi, r_own, r_ylo, r_yhi, r_xlo, r_xhi,
    q_out, w_out, r_out, e_out, r1_ref, low_ref, high_ref,
    q, w, r, e, c, e2, c2, diag, pairs, sems,
):
    boxed = box_parity
    q[0:6] = q_xlo[0:288].reshape(6, 48, 256)
    q[22:28] = q_xhi[0:288].reshape(6, 48, 256)
    q[6:22, 0:8] = q_ylo[0:16]
    q[6:22, 8:40] = q_own[...]
    q[6:22, 40:48] = q_yhi[0:16]
    r[1:6] = r_xlo[...]
    r[22:27] = r_xhi[...]
    r[6:22, 0:8] = r_ylo[...]
    r[6:22, 8:40] = r_own[...]
    r[6:22, 40:48] = r_yhi[...]
    pairs_out = ((q, q_out), (r, r_out), (w, w_out), (e, e_out))
    copies = [pltpu.make_async_copy(a, b, sems.at[i]) for i, (a, b) in enumerate(pairs_out)]
    copies[0].start()
    copies[1].start()
    set_weights(q, w, diag, 1, 27, boxed)
    copies[2].start()
    first_guess(e, c, q, w, r, 1, 27)
    sweep(e, c, e2, c2, q, w, r, 2, 26, boxed, unroll=8)
    sweep(e2, c2, e, c, q, w, r, 3, 25, boxed, unroll=8)
    copies[3].start()

    def left(x):
        return (r[x] + flow(e, c, q, x, boxed) - diag[x] * e[x])[8:40]

    def body(i, carry):
        pairs[i] = left(6 + 2 * i) + left(7 + 2 * i)
        return carry

    lax.fori_loop(0, 8, body, 0, unroll=4)
    r1 = 0.5 * halve(pairs[...]).reshape(8, 16, 128)
    r1_ref[...] = r1
    low_ref[...] = r1[:, :8]
    high_ref[...] = r1[:, 8:]
    for copy in copies:
        copy.wait()


def down_one_kernel(
    own, xlo, xhi, q_own, q_xlo, q_xhi,
    q, w, r, e, out_ref,
    c, e2, c2, diag, pairs,
):
    z = iota((32, 128), 1)
    boxed = functools.partial(box, z=z, depth=128)
    for i, side in enumerate((xlo, own, xhi)):
        r[8 * i : 8 * i + 8] = side[...]
    for i, side in enumerate((q_xlo[288:416].reshape(4, 32, 256), q_own[...], q_xhi[288:416].reshape(4, 32, 256))):
        q[8 * i : 8 * i + 4] = side[:, :, :128]
        q[8 * i + 4 : 8 * i + 8] = side[:, :, 128:]
    set_weights(q, w, diag, 1, 23, boxed)
    first_guess(e, c, q, w, r, 1, 23)
    sweep(e, c, e2, c2, q, w, r, 2, 22, boxed, unroll=8)
    sweep(e2, c2, e, c, q, w, r, 3, 21, boxed, unroll=8)

    def left(x):
        return (r[x] + flow(e, c, q, x, boxed) - diag[x] * e[x])[8:24]

    def body(i, carry):
        pairs[i] = left(8 + 2 * i) + left(9 + 2 * i)
        return carry

    lax.fori_loop(0, 4, body, 0, unroll=4)
    r2 = 0.5 * pack_two(pairs[...])
    out_ref[...] = jnp.broadcast_to(r2[None], (CHIPS, 16, 128))


def ghosts(ref, count, group):
    lane = iota((ref.shape[1], 128), 1)
    for at in range(0, ref.shape[2], 128):
        half = slice(at, at + 128)
        ref[0, :, half] = jnp.where(lane >= group, pltpu.roll(ref[count, :, half], group, axis=1), 0.0)
        ref[count + 1, :, half] = jnp.where(
            lane < 128 - group, pltpu.roll(ref[1, :, half], 128 - group, axis=1), 0.0
        )


def assemble_two(block, ref):
    lane = iota((16, 128), 1)
    low_half, low_quarter = lane < 64, (lane & 63) < 32

    def moved(x, by):
        return pltpu.roll(x, by, axis=1)

    def body(by, carry):
        rows = pl.ds(pl.multiple_of(by * 8, 8), 8)
        for h in range(2):
            a = [block(h, g, by) for g in range(4)]
            b = [None] * 4
            for i in range(2):
                b[i] = jnp.where(low_half, a[i], moved(a[i + 2], 64))
                b[i + 2] = jnp.where(low_half, moved(a[i], 64), a[i + 2])
            for i in (0, 2):
                first = jnp.where(low_quarter, b[i], moved(b[i + 1], 32))
                second = jnp.where(low_quarter, moved(b[i], 96), b[i + 1])
                for j, plane in ((i, first), (i + 1, second)):
                    ref[1 + h * 4 + j, rows, 0:128] = plane[0:8]
                    ref[1 + h * 4 + j, rows, 128:256] = plane[8:16]
        return carry

    lax.fori_loop(0, NY, body, 0, unroll=4)


def coarse_planes(planes):
    wide = jnp.concatenate([p[:, :128] + p[:, 128:] for p in planes], axis=1)
    thin = dot_split(pair_rows(64, 128), wide)
    return [thin[:, 128 * i : 128 * i + 128] for i in range(4)]


def boxes():
    z3, rows3 = iota((64, 128), 1) % 32, iota((64, 128), 0)
    return (
        functools.partial(box_parity, group=32, rows=iota((128, 256), 0)),
        functools.partial(box, z=z3, depth=32, rows=rows3),
    )


def setup_kernel(q2_all, q2, w2, d2, q3, w3):
    boxed2, boxed3 = boxes()
    assemble_two(lambda core, g, by: q2_all[(2 * g + core) * NY + by], q2)
    ghosts(q2, 8, 32)
    set_weights(q2, w2, d2, 1, 9, boxed2)
    for x, plane in enumerate(coarse_planes([q2[1 + 2 * x] + q2[2 + 2 * x] for x in range(4)])):
        q3[1 + x] = 0.125 * plane
    ghosts(q3, 4, 32)
    set_weights(q3, w3, None, 1, 5, boxed3)


def up_kernel(
    place_ref, r2_mine, r2_other, q2, w2, d2, q3, w3, *refs
):
    hbm, (grid_ref, back_ref) = refs[:11], refs[11:13]
    (
        r2, a2, ca2, b2, cb2,
        r3, a3, ca3, b3, cb3,
        last2, s1, c1, t1, ct1, s0, c0, t0, ct0, hi_ref, lo_ref, slots_ref, last0,
    ) = refs[13:36]
    local, sems = refs[36:47], refs[47]
    copies = [pltpu.make_async_copy(hbm[i], local[i], sems.at[i]) for i in range(11)]
    for copy in copies:
        copy.start()
    q1, w1, r1, e1, q0, w0, r0, e0, column_ref, depth_ref, factor_ref = local
    bx, by = place_ref[0], place_ref[1]
    boxed2, boxed3 = boxes()
    core = lax.rem(bx, 2)

    def block(of, g, by):
        i = g * NY + by
        return jnp.where(core == of, r2_mine[i], r2_other[i])

    assemble_two(block, r2)
    first_guess(a2, ca2, q2, w2, r2, 1, 9)

    def sweep2(e, c, e_to, c_to):
        ghosts(e, 8, 32)
        ghosts(c, 8, 32)
        sweep(e, c, e_to, c_to, q2, w2, r2, 1, 9, boxed2)

    sweep2(a2, ca2, b2, cb2)
    sweep2(b2, cb2, a2, ca2)
    ghosts(a2, 8, 32)
    ghosts(ca2, 8, 32)

    def left(x):
        return r2[x] + flow(a2, ca2, q2, x, boxed2) - d2[x] * a2[x]

    for x, plane in enumerate(coarse_planes([left(1 + 2 * x) + left(2 + 2 * x) for x in range(4)])):
        r3[1 + x] = 0.5 * plane
    first_guess(a3, ca3, q3, w3, r3, 1, 5)
    now, later = (a3, ca3), (b3, cb3)
    for _ in range(7):
        ghosts(now[0], 4, 32)
        ghosts(now[1], 4, 32)
        sweep(*now, *later, q3, w3, r3, 1, 5, boxed3)
        now, later = later, now
    e3 = now[0]
    rows_double = as_bf16(iota((128, 64), 0) // 2 == iota((128, 64), 1))
    more = dot_split(rows_double, jnp.concatenate([e3[1 + x] for x in range(4)], axis=1))
    for j in range(1, 9):
        add = more[:, (j - 1) // 2 * 128 : (j - 1) // 2 * 128 + 128]
        new = a2[j] + jnp.concatenate([add, add], axis=1)
        a2[j] = new
        ca2[j] = q2[j] * new
    sweep2(a2, ca2, b2, cb2)
    sweep2(b2, cb2, a2, ca2)
    ghosts(a2, 8, 32)
    ghosts(ca2, 8, 32)
    last2[:, 0:8] = jnp.zeros((8, 8, 256), F32)
    last2[:, 136:144] = jnp.zeros((8, 8, 256), F32)

    def final2(x, carry):
        last2[x - 1, 8:136] = 0.4 * a2[x] + w2[x] * (r2[x] + flow(a2, ca2, q2, x, boxed2))
        return carry

    lax.fori_loop(1, 9, final2, 0, unroll=2)
    z1 = iota((32, 128), 1)
    boxed1 = functools.partial(box, z=z1, depth=128)
    src, dst = iota((256, 128), 0), iota((256, 128), 1)
    widen_lanes = as_bf16(jnp.logical_and(dst // 4 == src % 128, dst // 2 % 2 == src // 128))
    widen_rows = as_bf16((iota((32, 24), 0) + 8) // 2 == iota((32, 24), 1))
    windows = []
    for j in range(10):
        x = bx * 4 - 3 + j
        inside = jnp.logical_and(x >= 0, x < 32)
        at = jnp.clip(x, 0, 31)
        rows = pl.ds(pl.multiple_of(by * 8, 8), 24)
        shift = lax.rem(128 - at // 8 * 32, 128)
        halves = [
            pltpu.roll(last2[lax.rem(at, 8), rows, lanes : lanes + 128], shift, axis=1) for lanes in (0, 128)
        ]
        windows.append(jnp.where(inside, jnp.concatenate(halves, axis=1), 0.0))
    wide = split_dot(jnp.concatenate(windows, axis=0), widen_lanes)
    wide = jnp.concatenate([wide[24 * j : 24 * j + 24] for j in range(10)], axis=1)
    wide = dot_split(widen_rows, wide)
    for copy in copies[:4]:
        copy.wait()
    for p in range(3, 21):
        j = (p - 2) // 2
        new = e1[p] + wide[:, 128 * j : 128 * j + 128]
        s1[p] = new
        c1[p] = q1[p] * new
    sweep(s1, c1, t1, ct1, q1, w1, r1, 4, 20, boxed1)
    sweep(t1, ct1, s1, c1, q1, w1, r1, 5, 19, boxed1)
    sweep(s1, c1, t1, None, q1, w1, r1, 6, 18, boxed1)
    boxed0 = box_parity
    wide_rows = as_bf16((iota((48, 32), 0) + 8) // 2 == iota((48, 32), 1))

    wide = dot_split(wide_rows, jnp.concatenate([t1[6 + j] for j in range(12)], axis=1))
    for copy in copies[4:]:
        copy.wait()
    for p in range(3, 25):
        add = wide[:, (p - 2) // 2 * 128 : (p - 2) // 2 * 128 + 128]
        new = e0[p] + jnp.concatenate([add, add], axis=1)
        s0[p] = new
        c0[p] = q0[p] * new
    sweep(s0, c0, t0, ct0, q0, w0, r0, 4, 24, boxed0)
    sweep(t0, ct0, s0, c0, q0, w0, r0, 5, 23, boxed0)

    def final0(x, carry):
        new = 0.4 * s0[x] + w0[x] * (r0[x] + flow(s0, c0, q0, x, boxed0))
        last0[x - 6] = new[8:40]
        return carry

    lax.fori_loop(6, 22, final0, 0, unroll=UNROLL)
    last = last0[...].reshape(512, 256)
    grid_ref[...] = split_dot(last, parity(1)).reshape(16, 32, 256)
    grid = jnp.transpose(last)
    up, down = scale_of(grid)
    hi, lo = two_parts(grid * up)
    hi_ref[...] = hi
    lo_ref[...] = lo.astype(F8)
    columns = iota16((512, CHUNK), 0)
    depths = iota((256, CHUNK), 0)

    def step(i, carry):
        at = pl.ds(pl.multiple_of(i * CHUNK, CHUNK), CHUNK)
        total = jnp.zeros((1, CHUNK), F32)
        for k in range(4):
            hot = hot16(columns, row16(column_ref[k : k + 1, at]))
            found = dot(hi_ref[...], hot) + dot(lo_ref[...], hot.astype(F8))
            here = depths == depth_lane(depth_ref[k : k + 1, at])
            picked = jnp.sum(jnp.where(here, found, 0.0), axis=0, keepdims=True)
            total = total + factor_ref[k : k + 1, at] * picked
        total = total * down
        for j in range(CHUNK // GROUP):
            slots_ref[pl.ds(i * (CHUNK // GROUP) + j, 1), :] = total[:, j * GROUP : (j + 1) * GROUP]
        return carry

    lax.fori_loop(0, SLOTS // CHUNK, step, 0)
    from_groups(slots_ref, back_ref)


def struct(*shape, dtype=F32):
    return jax.ShapeDtypeStruct(shape, dtype)


def call(kernel, outs, *args, smem=0, left=0, left_out=0, scratch=()):
    vmem = pl.BlockSpec(memory_space=pltpu.VMEM)
    return pl.pallas_call(
        kernel,
        out_shape=outs,
        in_specs=[pl.BlockSpec(memory_space=pltpu.SMEM)] * smem
        + [vmem] * (len(args) - smem - left)
        + [pl.BlockSpec(memory_space=pl.ANY)] * left,
        out_specs=tuple(pl.BlockSpec(memory_space=pl.ANY) if i < left_out else vmem for i in range(len(outs))),
        scratch_shapes=[pltpu.VMEM(s, d) for s, d in scratch]
        + ([pltpu.VMEM(a.shape, a.dtype) for a in args[-left:]] + [pltpu.SemaphoreType.DMA((left,))] if left else [])
        + ([pltpu.SemaphoreType.DMA((left_out,))] if left_out else []),
        compiler_params=pltpu.CompilerParams(vmem_limit_bytes=VMEM_BYTES),
    )(*args)


def swap(to_lower, to_upper, axis, count):
    up = [(i, i + 1) for i in range(count - 1)]
    down = [(j, i) for i, j in up]
    return lax.ppermute(to_upper, axis, up), lax.ppermute(to_lower, axis, down)


def shards(values, dest, active, column, depth, factor, base, state):
    dest = dest.reshape(64, 128)
    outgoing, rank = call(
        rank_kernel,
        (struct(DEVICES, LANES), struct(64, 128, dtype=jnp.int32)),
        active, dest, values.reshape(64, 128),
        smem=1, scratch=(((DEVICES, 256), F32), ((DEVICES, LANES), F32)),
    )
    incoming = lax.all_to_all(outgoing, ALL, split_axis=0, concat_axis=0, tiled=True)
    q, q1, q_low, q_high, q2 = call(
        kappa_kernel,
        (struct(16, 32, 256), struct(4, 16, 256), struct(20, 8, 256), struct(20, 8, 256), struct(16, 128)),
        base, state,
    )
    q2_all = lax.all_gather(q2[None], ALL, axis=0, tiled=True)
    q_ylo, q_yhi = swap(q_low, q_high, "by", NY)

    def faces(lo, own, hi, planes):
        return jnp.concatenate([lo[planes], own[planes], hi[planes]], axis=1)

    q1_cat = faces(q_ylo[16:], q1, q_yhi[16:], slice(0, 4))

    def q_faces(planes):
        return jnp.concatenate([faces(q_ylo, q, q_yhi, planes).reshape(288, 256), q1_cat.reshape(128, 256)])

    q_xlo, q_xhi = swap(q_faces(slice(0, 6)), q_faces(slice(10, 16)), BX, NX)

    rhs, r_low, r_high = call(
        deposit_kernel,
        (struct(16, 32, 256), struct(16, 8, 256), struct(16, 8, 256)),
        incoming, column, depth, factor,
        scratch=(((512, 256), F32), ((32, GROUP), F32)),
    )
    r_ylo, r_yhi = swap(r_low, r_high, "by", NY)
    r_xlo, r_xhi = swap(
        faces(r_ylo, rhs, r_yhi, slice(0, 5)), faces(r_ylo, rhs, r_yhi, slice(11, 16)), BX, NX
    )

    ext0, ext1 = (28, 48, 256), (24, 32, 128)
    q0e, w0e, r0e, e0e, r1, low1, high1 = call(
        down_kernel,
        (struct(*ext0),) * 4 + (struct(8, 16, 128), struct(8, 8, 128), struct(8, 8, 128)),
        q, q_ylo, q_yhi, q_xlo, q_xhi, rhs, r_ylo, r_yhi, r_xlo, r_xhi,
        left_out=4,
        scratch=((ext0, F32),) * 8 + (((8, 32, 256), F32),),
    )
    r1_ylo, r1_yhi = swap(low1, high1, "by", NY)
    cat1 = jnp.concatenate([r1_ylo, r1, r1_yhi], axis=1)
    xlo1, xhi1 = swap(cat1, cat1, BX, NX)

    q1e, w1e, r1e, e1e, r2_out = call(
        down_one_kernel,
        (struct(*ext1),) * 4 + (struct(CHIPS, 16, 128),),
        cat1, xlo1, xhi1, q1_cat, q_xlo, q_xhi,
        scratch=((ext1, F32),) * 4 + (((4, 16, 128), F32),),
    )
    q2_all, r2_out = lax.optimization_barrier((q2_all, r2_out))
    r2_mine = lax.all_to_all(r2_out, ("x", "by"), split_axis=0, concat_axis=0, tiled=True)
    whole2, whole3 = (10, 128, 256), (6, 64, 128)
    setup = call(setup_kernel, (struct(*whole2),) * 3 + (struct(*whole3),) * 2, q2_all)
    place = jnp.stack([lax.axis_index(BX), lax.axis_index("by")]).astype(jnp.int32)
    r2_mine, setup, place = lax.optimization_barrier((r2_mine, setup, place))
    r2_other = lax.ppermute(r2_mine, "core", [(0, 1), (1, 0)])

    grid, back = call(
        up_kernel,
        (struct(16, 32, 256), struct(DEVICES, LANES)),
        place, r2_mine, r2_other, *setup, q1e, w1e, r1e, e1e, q0e, w0e, r0e, e0e, column, depth, factor,
        smem=1,
        left=11,
        scratch=((whole2, F32),) * 5
        + ((whole3, F32),) * 5
        + (((8, 144, 256), F32),)
        + ((ext1, F32),) * 4
        + ((ext0, F32),) * 4
        + (((256, 512), BF16), ((256, 512), F8), ((32, GROUP), F32), ((16, 32, 256), F32)),
    )
    returned = lax.all_to_all(back, ALL, split_axis=0, concat_axis=0, tiled=True)
    (picked,) = call(pick_kernel, (struct(64, 128),), active, dest, rank, returned, smem=1)
    return grid, picked.reshape(ROWS)


def solution(mesh):
    placed = (
        P(ALL),
        P(ALL, None),
        P(ALL),
        P(None, ALL),
        P(None, ALL),
        P(None, ALL),
        P(BX, "by", None),
        P(BX, "by", None),
    )
    mesh = Mesh(mesh.devices.reshape(NX // 2, 2, NY), ALL)
    return jax.shard_map(
        shards,
        mesh=mesh,
        in_specs=placed,
        out_specs=(P(BX, "by", None), P(ALL)),
        check_vma=False,
    )
```
